32 devices in a mesh: seq: 16 (over z, y, core), head: 2 (over x).
Axes of the slice: x: 2, y: 2, z: 4, core: 2. Of those that a mesh axis runs over, the one named last changes fastest.
Arguments:
- queries: bfloat16 [2048, 3072], P(('seq', 'head')), may hold values from -6 to 6
- keys: bfloat16 [2048, 3072], P(('seq', 'head')), may hold values from -6 to 6
- values: bfloat16 [2048, 3072], P(('seq', 'head')), may hold values from -6 to 6
- counts: int32 [4], replicated, may hold values from 256 to 512, as said below
- plan: int32 [4], replicated, may hold values from 0 to 7
- group_mask: int32 [4, 4], replicated, may hold values from 0 to 1, as said below
- gate_table: float32 [8, 3072], replicated, may hold values from -6 to 6
Outputs:
- attended: bfloat16 [2048, 3072], P(('seq', 'head'))
The draws below stay inside these ranges and needn't reach their ends.
Inputs may be any that keep to these rules, and one draw needn't show every extreme that they name: `counts`: every group's count is at least half of 512; some group is full. `group_mask`: the diagonal is 1 and every entry above it is 0.
All inputs are finite; a program needn't handle non-finite values.
Results may differ from the reference program's by a relative error of at most 0.0046.
Values may be sent and summed in bfloat16 or wider, within the bound.
No kernel may reach another device: no remote copies, remote signals or barrier semaphores. Data moves between devices by JAX's collectives and lax.ppermute only.
A program may use at most 128 MiB of HBM per device.

```python
import math
import jax
import jax.numpy as jnp
from jax import lax

HEADS_WIN = 24
HEAD_DIM = 128
GROUPS = 4
LEVELS = 8
TOKENS = 2048
GROUP_TOK = 512
FEAT = 3072


def draw_queries(key, part):
    key = jax.random.fold_in(key, 11)
    base = jnp.clip(jax.random.normal(key, (TOKENS, HEADS_WIN * HEAD_DIM), jnp.float32), -6.0, 6.0)
    return base.astype(jnp.bfloat16)


def draw_keys(key, part):
    key = jax.random.fold_in(key, 12)
    base = jnp.clip(jax.random.normal(key, (TOKENS, HEADS_WIN * HEAD_DIM), jnp.float32), -6.0, 6.0)
    return base.astype(jnp.bfloat16)


def draw_counts(key, part):
    key = jax.random.fold_in(key, 21)
    first, second = jax.random.split(key)
    drawn = jax.random.randint(first, (GROUPS,), GROUP_TOK // 2, GROUP_TOK + 1)
    full = jax.random.randint(second, (), 0, GROUPS)
    return jnp.where(jnp.arange(GROUPS) == full, GROUP_TOK, drawn).astype(jnp.int32)


def draw_group_mask(key, part):
    key = jax.random.fold_in(key, 31)
    lower = jax.random.randint(key, (GROUPS, GROUPS), 0, 2)
    row_ids = jnp.arange(GROUPS)[:, None]
    col_ids = jnp.arange(GROUPS)[None, :]
    return jnp.where(row_ids == col_ids, 1, jnp.where(col_ids < row_ids, lower, 0)).astype(jnp.int32)


def place_ends(entries, key, smallest, largest):
    dims = entries.shape
    index_at = [jax.random.randint(jax.random.fold_in(key, axis), (), 0, dims[axis]) for axis in range(len(dims))]
    entries = entries.at[tuple(index_at)].set(smallest)
    longest = dims.index(max(dims))
    index_at[longest] = (index_at[longest] + 1) % dims[longest]
    return entries.at[tuple(index_at)].set(largest)


def level_of(rng, extent, cuts, low, high):
    factor_of = 1.0
    for dim, parts in cuts:
        draws = jax.random.uniform(jax.random.fold_in(jax.random.fold_in(rng, 6), dim), (parts,), jnp.float32, low / len(cuts), high / len(cuts))
        factor_of = factor_of * jnp.repeat(jnp.exp(draws), extent[dim] // parts).reshape((-1,) + (1,) * (len(extent) - 1 - dim))
    return factor_of


def noise(rng, extent, width, most, pieces=(), held_as=jnp.bfloat16):
    array = jax.random.normal(rng, extent, jnp.float32) * width
    if len(pieces) > 0:
        array = level_of(rng, extent, pieces, -0.22, 0.18) * array
    return jnp.clip(array, min=-most, max=most).astype(held_as)


def setup_inputs(seed: int = 0) -> dict:
    streams_of = jax.random.split(jax.random.key(seed), 8)
    queries = draw_queries(jax.random.fold_in(streams_of[7], 71), 0)
    keys = draw_keys(jax.random.fold_in(streams_of[7], 71), 0)
    values = noise(streams_of[2], (TOKENS, FEAT), 1.0, 6.0, ((0, 32),))
    counts = draw_counts(jax.random.fold_in(streams_of[7], 71), 0)
    plan = place_ends(jax.random.randint(streams_of[4], (GROUPS,), 0, LEVELS), jax.random.fold_in(streams_of[4], 1), 0, LEVELS - 1).astype(jnp.int32)
    group_mask = draw_group_mask(jax.random.fold_in(streams_of[7], 71), 0)
    gate_table = noise(streams_of[6], (LEVELS, FEAT), 1.0, 6.0, (), jnp.float32)
    return {"queries": queries, "keys": keys, "values": values, "counts": counts, "plan": plan, "group_mask": group_mask, "gate_table": gate_table}


def reference(queries, keys, values, counts, plan, group_mask, gate_table):
    block = math.gcd(TOKENS, 512)
    scale = 1.0 / math.sqrt(HEAD_DIM)
    rows = jnp.arange(TOKENS, dtype=jnp.int32)
    group_of = rows // GROUP_TOK
    position = rows % GROUP_TOK
    key_valid = position < counts[group_of]
    q_heads = jnp.transpose(queries.astype(jnp.float32).reshape(TOKENS, HEADS_WIN, HEAD_DIM), (1, 0, 2))
    k_heads = jnp.transpose(keys.astype(jnp.float32).reshape(TOKENS, HEADS_WIN, HEAD_DIM), (1, 0, 2))
    v_heads = jnp.transpose(values.reshape(TOKENS, HEADS_WIN, HEAD_DIM), (1, 0, 2))

    def one_block(start):
        q_group = lax.dynamic_slice_in_dim(group_of, start, block, 0)
        allowed = (group_mask[q_group][:, group_of] == 1) & key_valid[None, :]

        def one_head(items):
            q_all, k_all, v_all = items
            q_rows = lax.dynamic_slice_in_dim(q_all, start, block, 0)
            scores = jnp.dot(q_rows, k_all.T, precision=lax.Precision.HIGHEST) * scale
            scores = jnp.where(allowed, scores, jnp.float32(-1e+30))
            top = lax.optimization_barrier(jnp.max(scores, axis=1, keepdims=True))
            weights = jnp.exp(scores - top) * allowed.astype(jnp.float32)
            total = lax.optimization_barrier(jnp.sum(weights, axis=1, keepdims=True))
            rounded = weights.astype(jnp.bfloat16)
            return jnp.dot(rounded, v_all, preferred_element_type=jnp.float32) / total
        mixed = lax.map(one_head, (q_heads, k_heads, v_heads))
        mixed = jnp.transpose(mixed, (1, 0, 2)).reshape(block, FEAT)
        q_pos = lax.dynamic_slice_in_dim(position, start, block, 0)
        gates = gate_table[plan[q_group]]
        live = q_pos < counts[q_group]
        return jnp.where(live[:, None], mixed * gates, jnp.float32(0.0)).astype(jnp.bfloat16)
    starts = jnp.arange(0, TOKENS, block, dtype=jnp.int32)
    return lax.map(one_block, starts).reshape(TOKENS, FEAT)
```

```python
import functools
import math

import jax
import jax.numpy as jnp
from jax import lax
from jax.experimental import pallas as pl
from jax.experimental.pallas import tpu as pltpu
from jax.sharding import PartitionSpec as P

HEAD_DIM = 128
GROUPS = 4
LEVELS = 8


def lookup(table, index):
    hits = index[:, None] == jnp.arange(table.shape[0], dtype=jnp.int32)[None, :]
    return jnp.sum(jnp.where(hits, table[None, :], 0), axis=1)


def attend(
    work_q, k_local, v_local, row_group, row_pos, counts, plan, group_mask, gate_slice, group_tok
):
    rows = work_q.shape[0]
    width = work_q.shape[1]
    heads_here = width // HEAD_DIM
    scale = 1.0 / math.sqrt(HEAD_DIM)
    q_three = work_q.reshape(rows, heads_here, HEAD_DIM)
    row_onehot = (row_group[:, None] == jnp.arange(GROUPS, dtype=jnp.int32)[None, :]).astype(
        jnp.float32
    )
    mask_rows = jnp.dot(row_onehot, group_mask.astype(jnp.float32))
    k_piece = lax.all_gather(k_local, "seq", axis=0, tiled=True)
    v_piece = lax.all_gather(v_local, "seq", axis=0, tiled=True)
    count = k_piece.shape[0]
    index = jnp.arange(count, dtype=jnp.int32)
    k_group = index // group_tok
    k_pos = index % group_tok
    k_onehot = (k_group[:, None] == jnp.arange(GROUPS, dtype=jnp.int32)[None, :]).astype(
        jnp.float32
    )
    k_valid = k_pos < lookup(counts, k_group)
    allowed = (jnp.dot(mask_rows, k_onehot.T) > 0.5) & k_valid[None, :]
    running = jnp.full((heads_here, rows), -1e30, jnp.float32)
    k_three = k_piece.reshape(count, heads_here, HEAD_DIM)
    v_three = v_piece.reshape(count, heads_here, HEAD_DIM)
    scores = (
        jnp.einsum("qhd,khd->hqk", q_three, k_three, preferred_element_type=jnp.float32) * scale
    )
    scores = jnp.where(allowed[None], scores, jnp.float32(-1e30))
    newest = jnp.maximum(running, jnp.max(scores, axis=2))
    weights = jnp.exp(scores - newest[:, :, None]) * allowed[None].astype(jnp.float32)
    total = jnp.sum(weights, axis=2)
    rounded = weights.astype(jnp.bfloat16)
    accum = jnp.einsum("hqk,khd->hqd", rounded, v_three, preferred_element_type=jnp.float32)
    running, total, accum = (newest, total, accum)
    mixed = accum / total[:, :, None]
    mixed = jnp.transpose(mixed, (1, 0, 2)).reshape(rows, width)
    level_rows = lookup(plan, row_group)
    level_hits = level_rows[:, None] == jnp.arange(LEVELS, dtype=jnp.int32)[None, :]
    gates = jnp.sum(
        jnp.where(level_hits[:, :, None], gate_slice[None, :, :], jnp.float32(0.0)), axis=1
    )
    live = row_pos < lookup(counts, row_group)
    return jnp.where(live[:, None], mixed * gates, jnp.float32(0.0)).astype(jnp.bfloat16)


def gathered(queries, keys, values, counts, plan, group_mask, gate_table):
    n_seq = lax.axis_size("seq")
    n_head = lax.axis_size("head")
    per_group = n_seq // GROUPS
    tok_dev = queries.shape[0] * n_head
    group_tok = tok_dev * per_group
    q_local, k_local, v_local = (
        lax.all_to_all(queries, "head", split_axis=1, concat_axis=0, tiled=True),
        lax.all_to_all(keys, "head", split_axis=1, concat_axis=0, tiled=True),
        lax.all_to_all(values, "head", split_axis=1, concat_axis=0, tiled=True),
    )
    width = q_local.shape[1]
    seq_index = lax.axis_index("seq")
    own_group = seq_index // per_group
    positions = seq_index % per_group * tok_dev + jnp.arange(tok_dev, dtype=jnp.int32)
    gate_slice = lax.dynamic_slice_in_dim(gate_table, lax.axis_index("head") * width, width, 1)
    row_group = jnp.full((tok_dev,), own_group, jnp.int32)
    result = attend(
        q_local,
        k_local,
        v_local,
        row_group,
        positions,
        counts,
        plan,
        group_mask,
        gate_slice,
        group_tok,
    )
    return lax.all_to_all(result, "head", split_axis=0, concat_axis=1, tiled=True)


def attention_kernel(block_q, counts_ref, plan_ref, mask_ref, place_ref, q_ref, k_ref, v_ref, gate_ref, out_ref):
    tokens = q_ref.shape[0]
    group_tok = tokens // GROUPS
    factor = math.log2(math.e) / math.sqrt(HEAD_DIM)
    head = place_ref[0]
    busy = place_ref[1]

    @pl.when(busy == 1)
    def _():
        gates = gate_ref[:, pl.ds(pl.multiple_of(head * HEAD_DIM, HEAD_DIM), HEAD_DIM)]
        level = lax.broadcasted_iota(jnp.int32, (LEVELS, HEAD_DIM), 0)
        for c in range(GROUPS):
            width = (c + 1) * group_tok
            column = lax.broadcasted_iota(jnp.int32, (1, group_tok), 1)
            limits = [counts_ref[d] * mask_ref[c, d] for d in range(c + 1)]
            allowed = jnp.concatenate([column < limits[d] for d in range(c + 1)], axis=1)
            gate = jnp.sum(jnp.where(level == plan_ref[c], gates, jnp.float32(0.0)), axis=0, keepdims=True)

            @pl.loop(0, group_tok // block_q)
            def _(step):
                row = pl.multiple_of(c * group_tok + step * block_q, block_q)
                scores = lax.dot_general(
                    q_ref[pl.ds(row, block_q), :],
                    k_ref[:width, :],
                    (((1,), (1,)), ((), ())),
                    preferred_element_type=jnp.float32,
                )
                scores = jnp.where(allowed, scores, jnp.float32(-1e30))
                top = jnp.max(scores, axis=1, keepdims=True)
                weights = jnp.exp2(scores * factor - top * factor)
                total = jnp.sum(weights, axis=1, keepdims=True)
                mixed = jnp.dot(
                    weights.astype(jnp.bfloat16), v_ref[:width, :], preferred_element_type=jnp.float32
                )
                position = step * block_q + lax.broadcasted_iota(jnp.int32, (block_q, 1), 0)
                mixed = mixed / total * gate
                out_ref[pl.ds(row, block_q), :] = jnp.where(
                    position < counts_ref[c], mixed, jnp.float32(0.0)
                ).astype(jnp.bfloat16)

    @pl.when(busy == 0)
    def _():
        out_ref[...] = jnp.zeros_like(out_ref)


def attention(q, k, v, counts, plan, group_mask, place, gate_table):
    tokens = q.shape[0]
    smem = pl.BlockSpec(memory_space=pltpu.SMEM)
    vmem = pl.BlockSpec(memory_space=pltpu.VMEM)
    return pl.pallas_call(
        functools.partial(attention_kernel, 256),
        out_shape=jax.ShapeDtypeStruct((tokens, HEAD_DIM), jnp.bfloat16),
        in_specs=[smem, smem, smem, smem, vmem, vmem, vmem, vmem],
        out_specs=vmem,
        compiler_params=pltpu.CompilerParams(vmem_limit_bytes=40 * 1024 * 1024),
    )(counts, plan, group_mask, place, q, k, v, gate_table)


def head_each(queries, keys, values, counts, plan, group_mask, gate_table):
    axes = ("seq", "head")
    n_dev = lax.axis_size("seq") * lax.axis_size("head")
    local = queries.shape[0]
    heads = queries.shape[1] // HEAD_DIM
    parts = math.gcd(heads, n_dev)
    held, slots = heads // parts, n_dev // parts
    index = lax.axis_index("seq") * lax.axis_size("head") + lax.axis_index("head")
    lane = index % slots
    busy = (lane < held).astype(jnp.int32)
    head = jnp.minimum(index // slots * held + lane, heads - 1)
    place = jnp.stack([head, busy]).astype(jnp.int32)

    def by_slot(x):
        x = jnp.transpose(x.reshape(local, parts, held, HEAD_DIM), (1, 2, 0, 3))
        return jnp.pad(x, ((0, 0), (0, slots - held), (0, 0), (0, 0)))

    sent = jnp.stack([by_slot(queries), by_slot(keys), by_slot(values)], axis=2)
    sent = sent.reshape(n_dev, 3, local, HEAD_DIM)
    got = lax.all_to_all(sent, axes, split_axis=0, concat_axis=0, tiled=True)
    q, k, v = (got[:, i].reshape(n_dev * local, HEAD_DIM) for i in range(3))
    result = attention(q, k, v, counts, plan, group_mask, place, gate_table)
    back = lax.all_to_all(
        result.reshape(n_dev, local, HEAD_DIM), axes, split_axis=0, concat_axis=0, tiled=True
    )
    back = back.reshape(parts, slots, local, HEAD_DIM)[:, :held]
    return jnp.transpose(back, (2, 0, 1, 3)).reshape(local, heads * HEAD_DIM)


def on_device(queries, keys, values, counts, plan, group_mask, gate_table):
    n_dev = lax.axis_size("seq") * lax.axis_size("head")
    heads = queries.shape[1] // HEAD_DIM
    plan_of = head_each if heads <= n_dev <= 2 * heads else gathered
    return plan_of(queries, keys, values, counts, plan, group_mask, gate_table)


def solution(mesh):
    in_specs = (
        P(("seq", "head"), None),
        P(("seq", "head"), None),
        P(("seq", "head"), None),
        P(),
        P(),
        P(),
        P(),
    )
    out_specs = P(("seq", "head"), None)
    return jax.shard_map(
        on_device, mesh=mesh, in_specs=in_specs, out_specs=out_specs, check_vma=False
    )
```

```python
import functools
import math

import jax
import jax.numpy as jnp
from jax import lax
from jax.experimental import pallas as pl
from jax.experimental.pallas import tpu as pltpu
from jax.sharding import PartitionSpec as P

HEAD_DIM = 128
GROUPS = 4
LEVELS = 8


def lookup(table, index):
    hits = index[:, None] == jnp.arange(table.shape[0], dtype=jnp.int32)[None, :]
    return jnp.sum(jnp.where(hits, table[None, :], 0), axis=1)


def attend(
    work_q, k_local, v_local, row_group, row_pos, counts, plan, group_mask, gate_slice, group_tok
):
    rows = work_q.shape[0]
    width = work_q.shape[1]
    heads_here = width // HEAD_DIM
    scale = 1.0 / math.sqrt(HEAD_DIM)
    q_three = work_q.reshape(rows, heads_here, HEAD_DIM)
    row_onehot = (row_group[:, None] == jnp.arange(GROUPS, dtype=jnp.int32)[None, :]).astype(
        jnp.float32
    )
    mask_rows = jnp.dot(row_onehot, group_mask.astype(jnp.float32))
    k_piece = lax.all_gather(k_local, "seq", axis=0, tiled=True)
    v_piece = lax.all_gather(v_local, "seq", axis=0, tiled=True)
    count = k_piece.shape[0]
    index = jnp.arange(count, dtype=jnp.int32)
    k_group = index // group_tok
    k_pos = index % group_tok
    k_onehot = (k_group[:, None] == jnp.arange(GROUPS, dtype=jnp.int32)[None, :]).astype(
        jnp.float32
    )
    k_valid = k_pos < lookup(counts, k_group)
    allowed = (jnp.dot(mask_rows, k_onehot.T) > 0.5) & k_valid[None, :]
    running = jnp.full((heads_here, rows), -1e30, jnp.float32)
    k_three = k_piece.reshape(count, heads_here, HEAD_DIM)
    v_three = v_piece.reshape(count, heads_here, HEAD_DIM)
    scores = (
        jnp.einsum("qhd,khd->hqk", q_three, k_three, preferred_element_type=jnp.float32) * scale
    )
    scores = jnp.where(allowed[None], scores, jnp.float32(-1e30))
    newest = jnp.maximum(running, jnp.max(scores, axis=2))
    weights = jnp.exp(scores - newest[:, :, None]) * allowed[None].astype(jnp.float32)
    total = jnp.sum(weights, axis=2)
    rounded = weights.astype(jnp.bfloat16)
    accum = jnp.einsum("hqk,khd->hqd", rounded, v_three, preferred_element_type=jnp.float32)
    running, total, accum = (newest, total, accum)
    mixed = accum / total[:, :, None]
    mixed = jnp.transpose(mixed, (1, 0, 2)).reshape(rows, width)
    level_rows = lookup(plan, row_group)
    level_hits = level_rows[:, None] == jnp.arange(LEVELS, dtype=jnp.int32)[None, :]
    gates = jnp.sum(
        jnp.where(level_hits[:, :, None], gate_slice[None, :, :], jnp.float32(0.0)), axis=1
    )
    live = row_pos < lookup(counts, row_group)
    return jnp.where(live[:, None], mixed * gates, jnp.float32(0.0)).astype(jnp.bfloat16)


def gathered(queries, keys, values, counts, plan, group_mask, gate_table):
    n_seq = lax.axis_size("seq")
    n_head = lax.axis_size("head")
    per_group = n_seq // GROUPS
    tok_dev = queries.shape[0] * n_head
    group_tok = tok_dev * per_group
    q_local, k_local, v_local = (
        lax.all_to_all(queries, "head", split_axis=1, concat_axis=0, tiled=True),
        lax.all_to_all(keys, "head", split_axis=1, concat_axis=0, tiled=True),
        lax.all_to_all(values, "head", split_axis=1, concat_axis=0, tiled=True),
    )
    width = q_local.shape[1]
    seq_index = lax.axis_index("seq")
    own_group = seq_index // per_group
    positions = seq_index % per_group * tok_dev + jnp.arange(tok_dev, dtype=jnp.int32)
    gate_slice = lax.dynamic_slice_in_dim(gate_table, lax.axis_index("head") * width, width, 1)
    row_group = jnp.full((tok_dev,), own_group, jnp.int32)
    result = attend(
        q_local,
        k_local,
        v_local,
        row_group,
        positions,
        counts,
        plan,
        group_mask,
        gate_slice,
        group_tok,
    )
    return lax.all_to_all(result, "head", split_axis=0, concat_axis=1, tiled=True)


def pack_kernel(parts, held, q_ref, k_ref, v_ref, out_ref):
    slots = out_ref.shape[0] // parts
    for p in range(parts):
        for s in range(slots):
            for i, ref in enumerate((q_ref, k_ref, v_ref)):
                if s < held:
                    h = p * held + s
                    out_ref[p * slots + s, i] = ref[:, h * HEAD_DIM : (h + 1) * HEAD_DIM]
                else:
                    out_ref[p * slots + s, i] = jnp.zeros(out_ref.shape[2:], out_ref.dtype)


def unpack_kernel(parts, held, in_ref, out_ref):
    slots = in_ref.shape[0] // parts
    for p in range(parts):
        for s in range(held):
            h = p * held + s
            out_ref[:, h * HEAD_DIM : (h + 1) * HEAD_DIM] = in_ref[p * slots + s]


def attention_kernel(block, counts_ref, plan_ref, mask_ref, place_ref, got_ref, gate_ref, out_ref):
    n_dev, _, local, _ = got_ref.shape
    per_group = n_dev // GROUPS
    group_tok = per_group * local
    rows = block * local
    factor = math.log2(math.e) / math.sqrt(HEAD_DIM)
    head = place_ref[0]
    busy = place_ref[1]

    @pl.when(busy == 1)
    def _():
        gates = gate_ref[:, pl.ds(pl.multiple_of(head * HEAD_DIM, HEAD_DIM), HEAD_DIM)]
        level = lax.broadcasted_iota(jnp.int32, (LEVELS, HEAD_DIM), 0)
        for c in range(GROUPS):
            width = (c + 1) * group_tok
            column = lax.broadcasted_iota(jnp.int32, (1, group_tok), 1)
            limits = [counts_ref[d] * mask_ref[c, d] for d in range(c + 1)]
            allowed = jnp.concatenate([column < limits[d] for d in range(c + 1)], axis=1)
            gate = jnp.sum(jnp.where(level == plan_ref[c], gates, jnp.float32(0.0)), axis=0, keepdims=True)

            @pl.loop(0, per_group // block)
            def _(step):
                first = c * per_group + step * block
                scores = lax.dot_general(
                    got_ref[pl.ds(first, block), 0].reshape(rows, HEAD_DIM),
                    got_ref[: (c + 1) * per_group, 1].reshape(width, HEAD_DIM),
                    (((1,), (1,)), ((), ())),
                    preferred_element_type=jnp.float32,
                )
                scores = jnp.where(allowed, scores, jnp.float32(-1e30))
                top = jnp.max(scores, axis=1, keepdims=True)
                weights = jnp.exp2(scores * factor - top * factor)
                total = jnp.sum(weights, axis=1, keepdims=True)
                mixed = jnp.dot(
                    weights.astype(jnp.bfloat16),
                    got_ref[: (c + 1) * per_group, 2].reshape(width, HEAD_DIM),
                    preferred_element_type=jnp.float32,
                )
                position = step * rows + lax.broadcasted_iota(jnp.int32, (rows, 1), 0)
                mixed = jnp.where(position < counts_ref[c], mixed / total * gate, jnp.float32(0.0))
                out_ref[pl.ds(first, block)] = mixed.astype(jnp.bfloat16).reshape(block, local, HEAD_DIM)

    @pl.when(busy == 0)
    def _():
        out_ref[...] = jnp.zeros_like(out_ref)


def head_each(queries, keys, values, counts, plan, group_mask, gate_table):
    axes = ("seq", "head")
    n_dev = lax.axis_size("seq") * lax.axis_size("head")
    local, feat = queries.shape
    heads = feat // HEAD_DIM
    parts = math.gcd(heads, n_dev)
    held, slots = heads // parts, n_dev // parts
    index = lax.axis_index("seq") * lax.axis_size("head") + lax.axis_index("head")
    lane = index % slots
    busy = (lane < held).astype(jnp.int32)
    head = jnp.minimum(index // slots * held + lane, heads - 1)
    place = jnp.stack([head, busy]).astype(jnp.int32)
    smem = pl.BlockSpec(memory_space=pltpu.SMEM)
    vmem = pl.BlockSpec(memory_space=pltpu.VMEM)

    sent = pl.pallas_call(
        functools.partial(pack_kernel, parts, held),
        out_shape=jax.ShapeDtypeStruct((n_dev, 3, local, HEAD_DIM), jnp.bfloat16),
        in_specs=[vmem] * 3,
        out_specs=vmem,
        compiler_params=pltpu.CompilerParams(vmem_limit_bytes=16 * 1024 * 1024),
        name="pack",
    )(queries, keys, values)
    got = lax.all_to_all(sent, axes, split_axis=0, concat_axis=0, tiled=True)
    result = pl.pallas_call(
        functools.partial(attention_kernel, max(1, 256 // local)),
        out_shape=jax.ShapeDtypeStruct((n_dev, local, HEAD_DIM), jnp.bfloat16),
        in_specs=[smem, smem, smem, smem, vmem, vmem],
        out_specs=vmem,
        compiler_params=pltpu.CompilerParams(vmem_limit_bytes=40 * 1024 * 1024),
        name="attention",
    )(counts, plan, group_mask, place, got, gate_table)
    back = lax.all_to_all(result, axes, split_axis=0, concat_axis=0, tiled=True)
    return pl.pallas_call(
        functools.partial(unpack_kernel, parts, held),
        out_shape=jax.ShapeDtypeStruct((local, feat), jnp.bfloat16),
        in_specs=[vmem],
        out_specs=vmem,
        compiler_params=pltpu.CompilerParams(vmem_limit_bytes=16 * 1024 * 1024),
        name="unpack",
    )(back)


def on_device(queries, keys, values, counts, plan, group_mask, gate_table):
    n_dev = lax.axis_size("seq") * lax.axis_size("head")
    heads = queries.shape[1] // HEAD_DIM
    plan_of = head_each if heads <= n_dev <= 2 * heads else gathered
    return plan_of(queries, keys, values, counts, plan, group_mask, gate_table)


def solution(mesh):
    in_specs = (
        P(("seq", "head"), None),
        P(("seq", "head"), None),
        P(("seq", "head"), None),
        P(),
        P(),
        P(),
        P(),
    )
    out_specs = P(("seq", "head"), None)
    return jax.shard_map(
        on_device, mesh=mesh, in_specs=in_specs, out_specs=out_specs, check_vma=False
    )
```

```python
import functools
import math

import jax
import jax.numpy as jnp
from jax import lax
from jax.experimental import pallas as pl
from jax.experimental.pallas import tpu as pltpu
from jax.sharding import PartitionSpec as P

HEAD_DIM = 128
GROUPS = 4
LEVELS = 8


def lookup(table, index):
    hits = index[:, None] == jnp.arange(table.shape[0], dtype=jnp.int32)[None, :]
    return jnp.sum(jnp.where(hits, table[None, :], 0), axis=1)


def attend(
    work_q, k_local, v_local, row_group, row_pos, counts, plan, group_mask, gate_slice, group_tok
):
    rows = work_q.shape[0]
    width = work_q.shape[1]
    heads_here = width // HEAD_DIM
    scale = 1.0 / math.sqrt(HEAD_DIM)
    q_three = work_q.reshape(rows, heads_here, HEAD_DIM)
    row_onehot = (row_group[:, None] == jnp.arange(GROUPS, dtype=jnp.int32)[None, :]).astype(
        jnp.float32
    )
    mask_rows = jnp.dot(row_onehot, group_mask.astype(jnp.float32))
    k_piece = lax.all_gather(k_local, "seq", axis=0, tiled=True)
    v_piece = lax.all_gather(v_local, "seq", axis=0, tiled=True)
    count = k_piece.shape[0]
    index = jnp.arange(count, dtype=jnp.int32)
    k_group = index // group_tok
    k_pos = index % group_tok
    k_onehot = (k_group[:, None] == jnp.arange(GROUPS, dtype=jnp.int32)[None, :]).astype(
        jnp.float32
    )
    k_valid = k_pos < lookup(counts, k_group)
    allowed = (jnp.dot(mask_rows, k_onehot.T) > 0.5) & k_valid[None, :]
    running = jnp.full((heads_here, rows), -1e30, jnp.float32)
    k_three = k_piece.reshape(count, heads_here, HEAD_DIM)
    v_three = v_piece.reshape(count, heads_here, HEAD_DIM)
    scores = (
        jnp.einsum("qhd,khd->hqk", q_three, k_three, preferred_element_type=jnp.float32) * scale
    )
    scores = jnp.where(allowed[None], scores, jnp.float32(-1e30))
    newest = jnp.maximum(running, jnp.max(scores, axis=2))
    weights = jnp.exp(scores - newest[:, :, None]) * allowed[None].astype(jnp.float32)
    total = jnp.sum(weights, axis=2)
    rounded = weights.astype(jnp.bfloat16)
    accum = jnp.einsum("hqk,khd->hqd", rounded, v_three, preferred_element_type=jnp.float32)
    running, total, accum = (newest, total, accum)
    mixed = accum / total[:, :, None]
    mixed = jnp.transpose(mixed, (1, 0, 2)).reshape(rows, width)
    level_rows = lookup(plan, row_group)
    level_hits = level_rows[:, None] == jnp.arange(LEVELS, dtype=jnp.int32)[None, :]
    gates = jnp.sum(
        jnp.where(level_hits[:, :, None], gate_slice[None, :, :], jnp.float32(0.0)), axis=1
    )
    live = row_pos < lookup(counts, row_group)
    return jnp.where(live[:, None], mixed * gates, jnp.float32(0.0)).astype(jnp.bfloat16)


def gathered(queries, keys, values, counts, plan, group_mask, gate_table):
    n_seq = lax.axis_size("seq")
    n_head = lax.axis_size("head")
    per_group = n_seq // GROUPS
    tok_dev = queries.shape[0] * n_head
    group_tok = tok_dev * per_group
    q_local, k_local, v_local = (
        lax.all_to_all(queries, "head", split_axis=1, concat_axis=0, tiled=True),
        lax.all_to_all(keys, "head", split_axis=1, concat_axis=0, tiled=True),
        lax.all_to_all(values, "head", split_axis=1, concat_axis=0, tiled=True),
    )
    width = q_local.shape[1]
    seq_index = lax.axis_index("seq")
    own_group = seq_index // per_group
    positions = seq_index % per_group * tok_dev + jnp.arange(tok_dev, dtype=jnp.int32)
    gate_slice = lax.dynamic_slice_in_dim(gate_table, lax.axis_index("head") * width, width, 1)
    row_group = jnp.full((tok_dev,), own_group, jnp.int32)
    result = attend(
        q_local,
        k_local,
        v_local,
        row_group,
        positions,
        counts,
        plan,
        group_mask,
        gate_slice,
        group_tok,
    )
    return lax.all_to_all(result, "head", split_axis=0, concat_axis=1, tiled=True)


def pack_kernel(held, slots, place_ref, q_ref, k_ref, v_ref, *out_refs):
    n_dev = len(out_refs)
    for step, out_ref in enumerate(out_refs):
        dest = lax.rem(place_ref[2] + step, n_dev)
        head = lax.div(dest, slots) * held + jnp.minimum(lax.rem(dest, slots), held - 1)
        columns = pl.ds(pl.multiple_of(head * HEAD_DIM, HEAD_DIM), HEAD_DIM)
        for i, ref in enumerate((q_ref, k_ref, v_ref)):
            out_ref[i] = ref[:, columns]


def unpack_kernel(parts, held, in_ref, out_ref):
    slots = in_ref.shape[0] // parts
    for p in range(parts):
        for s in range(held):
            h = p * held + s
            out_ref[:, h * HEAD_DIM : (h + 1) * HEAD_DIM] = in_ref[p * slots + s]


def attention_kernel(block, counts_ref, plan_ref, mask_ref, place_ref, gate_ref, *refs):
    *in_refs, out_ref, got_ref = refs
    n_dev, _, local, _ = got_ref.shape
    per_group = n_dev // GROUPS
    group_tok = per_group * local
    rows = block * local
    factor = math.log2(math.e) / math.sqrt(HEAD_DIM)
    head = place_ref[0]
    busy = place_ref[1]

    @pl.when(busy == 1)
    def _():
        for step, in_ref in enumerate(in_refs):
            got_ref[lax.rem(place_ref[2] + n_dev - step, n_dev)] = in_ref[...]
        gates = gate_ref[:, pl.ds(pl.multiple_of(head * HEAD_DIM, HEAD_DIM), HEAD_DIM)]
        level = lax.broadcasted_iota(jnp.int32, (LEVELS, HEAD_DIM), 0)
        for c in range(GROUPS):
            width = (c + 1) * group_tok
            column = lax.broadcasted_iota(jnp.int32, (1, group_tok), 1)
            limits = [counts_ref[d] * mask_ref[c, d] for d in range(c + 1)]
            allowed = jnp.concatenate([column < limits[d] for d in range(c + 1)], axis=1)
            gate = jnp.sum(jnp.where(level == plan_ref[c], gates, jnp.float32(0.0)), axis=0, keepdims=True)

            @pl.loop(0, per_group // block)
            def _(step):
                first = c * per_group + step * block
                scores = lax.dot_general(
                    got_ref[pl.ds(first, block), 0].reshape(rows, HEAD_DIM),
                    got_ref[: (c + 1) * per_group, 1].reshape(width, HEAD_DIM),
                    (((1,), (1,)), ((), ())),
                    preferred_element_type=jnp.float32,
                )
                scores = jnp.where(allowed, scores, jnp.float32(-1e30))
                top = jnp.max(scores, axis=1, keepdims=True)
                weights = jnp.exp2(scores * factor - top * factor)
                total = jnp.sum(weights, axis=1, keepdims=True)
                mixed = jnp.dot(
                    weights.astype(jnp.bfloat16),
                    got_ref[: (c + 1) * per_group, 2].reshape(width, HEAD_DIM),
                    preferred_element_type=jnp.float32,
                )
                position = step * rows + lax.broadcasted_iota(jnp.int32, (rows, 1), 0)
                mixed = jnp.where(position < counts_ref[c], mixed / total * gate, jnp.float32(0.0))
                out_ref[pl.ds(first, block)] = mixed.astype(jnp.bfloat16).reshape(block, local, HEAD_DIM)

    @pl.when(busy == 0)
    def _():
        out_ref[...] = jnp.zeros_like(out_ref)


def head_each(queries, keys, values, counts, plan, group_mask, gate_table):
    axes = ("seq", "head")
    n_dev = lax.axis_size("seq") * lax.axis_size("head")
    local, feat = queries.shape
    heads = feat // HEAD_DIM
    parts = math.gcd(heads, n_dev)
    held, slots = heads // parts, n_dev // parts
    index = lax.axis_index("seq") * lax.axis_size("head") + lax.axis_index("head")
    lane = index % slots
    busy = (lane < held).astype(jnp.int32)
    head = jnp.minimum(index // slots * held + lane, heads - 1)
    place = jnp.stack([head, busy, index]).astype(jnp.int32)
    smem = pl.BlockSpec(memory_space=pltpu.SMEM)
    vmem = pl.BlockSpec(memory_space=pltpu.VMEM)

    piece = jax.ShapeDtypeStruct((3, local, HEAD_DIM), jnp.bfloat16)
    sent = pl.pallas_call(
        functools.partial(pack_kernel, held, slots),
        out_shape=[piece] * n_dev,
        in_specs=[smem] + [vmem] * 3,
        out_specs=[vmem] * n_dev,
        compiler_params=pltpu.CompilerParams(vmem_limit_bytes=16 * 1024 * 1024),
        name="pack",
    )(place, queries, keys, values)
    got = [sent[0]] * n_dev
    bits = (n_dev - 1).bit_length()
    order = sorted(range(1, n_dev), key=lambda step: format(step, f"0{bits}b")[::-1])
    for step in order:
        pairs = [(d, (d + step) % n_dev) for d in range(n_dev)]
        pairs = [(d, e) for d, e in pairs if e % slots < held]
        got[step] = lax.ppermute(sent[step], axes, pairs)
    result = pl.pallas_call(
        functools.partial(attention_kernel, max(1, 256 // local)),
        out_shape=jax.ShapeDtypeStruct((n_dev, local, HEAD_DIM), jnp.bfloat16),
        in_specs=[smem, smem, smem, smem, vmem] + [vmem] * n_dev,
        out_specs=vmem,
        scratch_shapes=[pltpu.VMEM((n_dev, 3, local, HEAD_DIM), jnp.bfloat16)],
        compiler_params=pltpu.CompilerParams(vmem_limit_bytes=40 * 1024 * 1024),
        name="attention",
    )(counts, plan, group_mask, place, gate_table, *got)
    back = lax.all_to_all(result, axes, split_axis=0, concat_axis=0, tiled=True)
    return pl.pallas_call(
        functools.partial(unpack_kernel, parts, held),
        out_shape=jax.ShapeDtypeStruct((local, feat), jnp.bfloat16),
        in_specs=[vmem],
        out_specs=vmem,
        compiler_params=pltpu.CompilerParams(vmem_limit_bytes=16 * 1024 * 1024),
        name="unpack",
    )(back)


def on_device(queries, keys, values, counts, plan, group_mask, gate_table):
    n_dev = lax.axis_size("seq") * lax.axis_size("head")
    heads = queries.shape[1] // HEAD_DIM
    plan_of = head_each if heads <= n_dev <= 2 * heads else gathered
    return plan_of(queries, keys, values, counts, plan, group_mask, gate_table)


def solution(mesh):
    in_specs = (
        P(("seq", "head"), None),
        P(("seq", "head"), None),
        P(("seq", "head"), None),
        P(),
        P(),
        P(),
        P(),
    )
    out_specs = P(("seq", "head"), None)
    return jax.shard_map(
        on_device, mesh=mesh, in_specs=in_specs, out_specs=out_specs, check_vma=False
    )
```

```python
import functools
import math

import jax
import jax.numpy as jnp
from jax import lax
from jax.experimental import pallas as pl
from jax.experimental.pallas import tpu as pltpu
from jax.sharding import PartitionSpec as P

HEAD_DIM = 128
GROUPS = 4
LEVELS = 8


def lookup(table, index):
    hits = index[:, None] == jnp.arange(table.shape[0], dtype=jnp.int32)[None, :]
    return jnp.sum(jnp.where(hits, table[None, :], 0), axis=1)


def attend(
    work_q, k_local, v_local, row_group, row_pos, counts, plan, group_mask, gate_slice, group_tok
):
    rows = work_q.shape[0]
    width = work_q.shape[1]
    heads_here = width // HEAD_DIM
    scale = 1.0 / math.sqrt(HEAD_DIM)
    q_three = work_q.reshape(rows, heads_here, HEAD_DIM)
    row_onehot = (row_group[:, None] == jnp.arange(GROUPS, dtype=jnp.int32)[None, :]).astype(
        jnp.float32
    )
    mask_rows = jnp.dot(row_onehot, group_mask.astype(jnp.float32))
    k_piece = lax.all_gather(k_local, "seq", axis=0, tiled=True)
    v_piece = lax.all_gather(v_local, "seq", axis=0, tiled=True)
    count = k_piece.shape[0]
    index = jnp.arange(count, dtype=jnp.int32)
    k_group = index // group_tok
    k_pos = index % group_tok
    k_onehot = (k_group[:, None] == jnp.arange(GROUPS, dtype=jnp.int32)[None, :]).astype(
        jnp.float32
    )
    k_valid = k_pos < lookup(counts, k_group)
    allowed = (jnp.dot(mask_rows, k_onehot.T) > 0.5) & k_valid[None, :]
    running = jnp.full((heads_here, rows), -1e30, jnp.float32)
    k_three = k_piece.reshape(count, heads_here, HEAD_DIM)
    v_three = v_piece.reshape(count, heads_here, HEAD_DIM)
    scores = (
        jnp.einsum("qhd,khd->hqk", q_three, k_three, preferred_element_type=jnp.float32) * scale
    )
    scores = jnp.where(allowed[None], scores, jnp.float32(-1e30))
    newest = jnp.maximum(running, jnp.max(scores, axis=2))
    weights = jnp.exp(scores - newest[:, :, None]) * allowed[None].astype(jnp.float32)
    total = jnp.sum(weights, axis=2)
    rounded = weights.astype(jnp.bfloat16)
    accum = jnp.einsum("hqk,khd->hqd", rounded, v_three, preferred_element_type=jnp.float32)
    running, total, accum = (newest, total, accum)
    mixed = accum / total[:, :, None]
    mixed = jnp.transpose(mixed, (1, 0, 2)).reshape(rows, width)
    level_rows = lookup(plan, row_group)
    level_hits = level_rows[:, None] == jnp.arange(LEVELS, dtype=jnp.int32)[None, :]
    gates = jnp.sum(
        jnp.where(level_hits[:, :, None], gate_slice[None, :, :], jnp.float32(0.0)), axis=1
    )
    live = row_pos < lookup(counts, row_group)
    return jnp.where(live[:, None], mixed * gates, jnp.float32(0.0)).astype(jnp.bfloat16)


def gathered(queries, keys, values, counts, plan, group_mask, gate_table):
    n_seq = lax.axis_size("seq")
    n_head = lax.axis_size("head")
    per_group = n_seq // GROUPS
    tok_dev = queries.shape[0] * n_head
    group_tok = tok_dev * per_group
    q_local, k_local, v_local = (
        lax.all_to_all(queries, "head", split_axis=1, concat_axis=0, tiled=True),
        lax.all_to_all(keys, "head", split_axis=1, concat_axis=0, tiled=True),
        lax.all_to_all(values, "head", split_axis=1, concat_axis=0, tiled=True),
    )
    width = q_local.shape[1]
    seq_index = lax.axis_index("seq")
    own_group = seq_index // per_group
    positions = seq_index % per_group * tok_dev + jnp.arange(tok_dev, dtype=jnp.int32)
    gate_slice = lax.dynamic_slice_in_dim(gate_table, lax.axis_index("head") * width, width, 1)
    row_group = jnp.full((tok_dev,), own_group, jnp.int32)
    result = attend(
        q_local,
        k_local,
        v_local,
        row_group,
        positions,
        counts,
        plan,
        group_mask,
        gate_slice,
        group_tok,
    )
    return lax.all_to_all(result, "head", split_axis=0, concat_axis=1, tiled=True)


def pack_kernel(parts, held, *refs):
    count = (len(refs) - 2) // 2
    in_refs, out_ref, bufs, sems = refs[:count], refs[count], refs[count + 1 : -1], refs[-1]
    slots = out_ref.shape[0] // parts
    copies = [pltpu.make_async_copy(in_refs[i], bufs[i], sems.at[i]) for i in range(count)]
    for copy in copies:
        copy.start()
    for s in range(held, slots):
        for p in range(parts):
            out_ref[p * slots + s] = jnp.zeros(out_ref.shape[1:], out_ref.dtype)
    for i, copy in enumerate(copies):
        copy.wait()
        for p in range(parts):
            for s in range(held):
                h = p * held + s
                out_ref[p * slots + s, i] = bufs[i][:, h * HEAD_DIM : (h + 1) * HEAD_DIM]


def pack(arrays, parts, held, n_dev):
    local, feat = arrays[0].shape
    count = len(arrays)
    return pl.pallas_call(
        functools.partial(pack_kernel, parts, held),
        out_shape=jax.ShapeDtypeStruct((n_dev, count, local, HEAD_DIM), jnp.bfloat16),
        in_specs=[pl.BlockSpec(memory_space=pl.ANY)] * count,
        out_specs=pl.BlockSpec(memory_space=pltpu.VMEM),
        scratch_shapes=[pltpu.VMEM((local, feat), jnp.bfloat16)] * count + [pltpu.SemaphoreType.DMA((count,))],
        compiler_params=pltpu.CompilerParams(vmem_limit_bytes=60 * 1024 * 1024),
        cost_estimate=pl.CostEstimate(flops=0, bytes_accessed=count * local * feat * 5, transcendentals=0),
        name="pack",
    )(*arrays)


def unpack_kernel(parts, held, in_ref, out_ref):
    slots = in_ref.shape[0] // parts
    for p in range(parts):
        for s in range(held):
            h = p * held + s
            out_ref[:, h * HEAD_DIM : (h + 1) * HEAD_DIM] = in_ref[p * slots + s]


def weights_kernel(block, counts_ref, mask_ref, place_ref, got_ref, weights_ref, total_ref):
    n_dev, _, local, _ = got_ref.shape
    per_group = n_dev // GROUPS
    group_tok = per_group * local
    rows = block * local
    factor = math.log2(math.e) / math.sqrt(HEAD_DIM)

    @pl.when(place_ref[1] == 1)
    def _():
        for c in range(GROUPS):
            width = (c + 1) * group_tok
            column = lax.broadcasted_iota(jnp.int32, (1, group_tok), 1)
            limits = [counts_ref[d] * mask_ref[c, d] for d in range(c + 1)]
            allowed = jnp.concatenate([column < limits[d] for d in range(c + 1)], axis=1)

            @pl.loop(0, per_group // block)
            def _(step):
                first = c * per_group + step * block
                scores = lax.dot_general(
                    got_ref[pl.ds(first, block), 0].reshape(rows, HEAD_DIM),
                    got_ref[: (c + 1) * per_group, 1].reshape(width, HEAD_DIM),
                    (((1,), (1,)), ((), ())),
                    preferred_element_type=jnp.float32,
                )
                scores = jnp.where(allowed, scores, jnp.float32(-1e30))
                top = jnp.max(scores, axis=1, keepdims=True)
                weights = jnp.exp2(scores * factor - top * factor)
                row = pl.multiple_of(step * rows, rows)
                total = jnp.sum(weights, axis=1, keepdims=True)
                total_ref[c, pl.ds(row, rows), :] = jnp.broadcast_to(total, (rows, HEAD_DIM))
                weights = weights.astype(jnp.bfloat16)
                for d in range(c + 1):
                    weights_ref[c * (c + 1) // 2 + d, pl.ds(row, rows), :] = weights[
                        :, d * group_tok : (d + 1) * group_tok
                    ]


def mix_kernel(counts_ref, plan_ref, place_ref, weights_ref, total_ref, v_ref, gate_ref, out_ref):
    n_dev, _, local, _ = v_ref.shape
    per_group = n_dev // GROUPS
    group_tok = per_group * local
    head = place_ref[0]
    busy = place_ref[1]

    @pl.when(busy == 1)
    def _():
        gates = gate_ref[:, pl.ds(pl.multiple_of(head * HEAD_DIM, HEAD_DIM), HEAD_DIM)]
        level = lax.broadcasted_iota(jnp.int32, (LEVELS, HEAD_DIM), 0)
        for c in range(GROUPS):
            gate = jnp.sum(jnp.where(level == plan_ref[c], gates, jnp.float32(0.0)), axis=0, keepdims=True)
            mixed = jnp.zeros((group_tok, HEAD_DIM), jnp.float32)
            for d in range(c + 1):
                mixed += jnp.dot(
                    weights_ref[c * (c + 1) // 2 + d],
                    v_ref[d * per_group : (d + 1) * per_group, 0].reshape(group_tok, HEAD_DIM),
                    preferred_element_type=jnp.float32,
                )
            position = lax.broadcasted_iota(jnp.int32, (group_tok, 1), 0)
            mixed = jnp.where(position < counts_ref[c], mixed / total_ref[c] * gate, jnp.float32(0.0))
            out_ref[c * per_group : (c + 1) * per_group] = mixed.astype(jnp.bfloat16).reshape(
                per_group, local, HEAD_DIM
            )

    @pl.when(busy == 0)
    def _():
        out_ref[...] = jnp.zeros_like(out_ref)


def head_each(queries, keys, values, counts, plan, group_mask, gate_table):
    axes = ("seq", "head")
    n_dev = lax.axis_size("seq") * lax.axis_size("head")
    local, feat = queries.shape
    heads = feat // HEAD_DIM
    parts = math.gcd(heads, n_dev)
    held, slots = heads // parts, n_dev // parts
    index = lax.axis_index("seq") * lax.axis_size("head") + lax.axis_index("head")
    lane = index % slots
    busy = (lane < held).astype(jnp.int32)
    head = jnp.minimum(index // slots * held + lane, heads - 1)
    place = jnp.stack([head, busy]).astype(jnp.int32)
    smem = pl.BlockSpec(memory_space=pltpu.SMEM)
    vmem = pl.BlockSpec(memory_space=pltpu.VMEM)

    got = lax.all_to_all(pack((queries, keys), parts, held, n_dev), axes, split_axis=0, concat_axis=0, tiled=True)
    got_v = lax.all_to_all(pack((values,), parts, held, n_dev), axes, split_axis=0, concat_axis=0, tiled=True)
    group_tok = n_dev * local // GROUPS
    pairs = GROUPS * (GROUPS + 1) // 2
    work = pairs * group_tok * group_tok
    weights, total = pl.pallas_call(
        functools.partial(weights_kernel, max(1, 256 // local)),
        out_shape=[
            jax.ShapeDtypeStruct((pairs, group_tok, group_tok), jnp.bfloat16),
            jax.ShapeDtypeStruct((GROUPS, group_tok, HEAD_DIM), jnp.float32),
        ],
        in_specs=[smem, smem, smem, vmem],
        out_specs=[vmem, vmem],
        compiler_params=pltpu.CompilerParams(vmem_limit_bytes=32 * 1024 * 1024),
        cost_estimate=pl.CostEstimate(flops=2 * work * HEAD_DIM, bytes_accessed=work * 4, transcendentals=work),
        name="weights",
    )(counts, group_mask, place, got)
    result = pl.pallas_call(
        mix_kernel,
        out_shape=jax.ShapeDtypeStruct((n_dev, local, HEAD_DIM), jnp.bfloat16),
        in_specs=[smem, smem, smem, vmem, vmem, vmem, vmem],
        out_specs=vmem,
        compiler_params=pltpu.CompilerParams(vmem_limit_bytes=32 * 1024 * 1024),
        cost_estimate=pl.CostEstimate(flops=2 * work * HEAD_DIM, bytes_accessed=work * 2, transcendentals=0),
        name="mix",
    )(counts, plan, place, weights, total, got_v, gate_table)
    back = lax.all_to_all(result, axes, split_axis=0, concat_axis=0, tiled=True)
    return pl.pallas_call(
        functools.partial(unpack_kernel, parts, held),
        out_shape=jax.ShapeDtypeStruct((local, feat), jnp.bfloat16),
        in_specs=[vmem],
        out_specs=vmem,
        compiler_params=pltpu.CompilerParams(vmem_limit_bytes=16 * 1024 * 1024),
        name="unpack",
    )(back)


def on_device(queries, keys, values, counts, plan, group_mask, gate_table):
    n_dev = lax.axis_size("seq") * lax.axis_size("head")
    heads = queries.shape[1] // HEAD_DIM
    plan_of = head_each if heads <= n_dev <= 2 * heads else gathered
    return plan_of(queries, keys, values, counts, plan, group_mask, gate_table)


def solution(mesh):
    in_specs = (
        P(("seq", "head"), None),
        P(("seq", "head"), None),
        P(("seq", "head"), None),
        P(),
        P(),
        P(),
        P(),
    )
    out_specs = P(("seq", "head"), None)
    return jax.shard_map(
        on_device, mesh=mesh, in_specs=in_specs, out_specs=out_specs, check_vma=False
    )
```

```python
import functools
import math

import jax
import jax.numpy as jnp
from jax import lax
from jax.experimental import pallas as pl
from jax.experimental.pallas import tpu as pltpu
from jax.sharding import PartitionSpec as P

HEAD_DIM = 128
GROUPS = 4
LEVELS = 8


def lookup(table, index):
    hits = index[:, None] == jnp.arange(table.shape[0], dtype=jnp.int32)[None, :]
    return jnp.sum(jnp.where(hits, table[None, :], 0), axis=1)


def attend(
    work_q, k_local, v_local, row_group, row_pos, counts, plan, group_mask, gate_slice, group_tok
):
    rows = work_q.shape[0]
    width = work_q.shape[1]
    heads_here = width // HEAD_DIM
    scale = 1.0 / math.sqrt(HEAD_DIM)
    q_three = work_q.reshape(rows, heads_here, HEAD_DIM)
    row_onehot = (row_group[:, None] == jnp.arange(GROUPS, dtype=jnp.int32)[None, :]).astype(
        jnp.float32
    )
    mask_rows = jnp.dot(row_onehot, group_mask.astype(jnp.float32))
    k_piece = lax.all_gather(k_local, "seq", axis=0, tiled=True)
    v_piece = lax.all_gather(v_local, "seq", axis=0, tiled=True)
    count = k_piece.shape[0]
    index = jnp.arange(count, dtype=jnp.int32)
    k_group = index // group_tok
    k_pos = index % group_tok
    k_onehot = (k_group[:, None] == jnp.arange(GROUPS, dtype=jnp.int32)[None, :]).astype(
        jnp.float32
    )
    k_valid = k_pos < lookup(counts, k_group)
    allowed = (jnp.dot(mask_rows, k_onehot.T) > 0.5) & k_valid[None, :]
    running = jnp.full((heads_here, rows), -1e30, jnp.float32)
    k_three = k_piece.reshape(count, heads_here, HEAD_DIM)
    v_three = v_piece.reshape(count, heads_here, HEAD_DIM)
    scores = (
        jnp.einsum("qhd,khd->hqk", q_three, k_three, preferred_element_type=jnp.float32) * scale
    )
    scores = jnp.where(allowed[None], scores, jnp.float32(-1e30))
    newest = jnp.maximum(running, jnp.max(scores, axis=2))
    weights = jnp.exp(scores - newest[:, :, None]) * allowed[None].astype(jnp.float32)
    total = jnp.sum(weights, axis=2)
    rounded = weights.astype(jnp.bfloat16)
    accum = jnp.einsum("hqk,khd->hqd", rounded, v_three, preferred_element_type=jnp.float32)
    running, total, accum = (newest, total, accum)
    mixed = accum / total[:, :, None]
    mixed = jnp.transpose(mixed, (1, 0, 2)).reshape(rows, width)
    level_rows = lookup(plan, row_group)
    level_hits = level_rows[:, None] == jnp.arange(LEVELS, dtype=jnp.int32)[None, :]
    gates = jnp.sum(
        jnp.where(level_hits[:, :, None], gate_slice[None, :, :], jnp.float32(0.0)), axis=1
    )
    live = row_pos < lookup(counts, row_group)
    return jnp.where(live[:, None], mixed * gates, jnp.float32(0.0)).astype(jnp.bfloat16)


def gathered(queries, keys, values, counts, plan, group_mask, gate_table):
    n_seq = lax.axis_size("seq")
    n_head = lax.axis_size("head")
    per_group = n_seq // GROUPS
    tok_dev = queries.shape[0] * n_head
    group_tok = tok_dev * per_group
    q_local, k_local, v_local = (
        lax.all_to_all(queries, "head", split_axis=1, concat_axis=0, tiled=True),
        lax.all_to_all(keys, "head", split_axis=1, concat_axis=0, tiled=True),
        lax.all_to_all(values, "head", split_axis=1, concat_axis=0, tiled=True),
    )
    width = q_local.shape[1]
    seq_index = lax.axis_index("seq")
    own_group = seq_index // per_group
    positions = seq_index % per_group * tok_dev + jnp.arange(tok_dev, dtype=jnp.int32)
    gate_slice = lax.dynamic_slice_in_dim(gate_table, lax.axis_index("head") * width, width, 1)
    row_group = jnp.full((tok_dev,), own_group, jnp.int32)
    result = attend(
        q_local,
        k_local,
        v_local,
        row_group,
        positions,
        counts,
        plan,
        group_mask,
        gate_slice,
        group_tok,
    )
    return lax.all_to_all(result, "head", split_axis=0, concat_axis=1, tiled=True)


def pack_kernel(parts, held, *refs):
    count = (len(refs) - 2) // 2
    in_refs, out_ref, bufs, sems = refs[:count], refs[count], refs[count + 1 : -1], refs[-1]
    slots = out_ref.shape[0] // parts
    copies = [pltpu.make_async_copy(in_refs[i], bufs[i], sems.at[i]) for i in range(count)]
    for copy in copies:
        copy.start()
    for s in range(held, slots):
        for p in range(parts):
            out_ref[p * slots + s] = jnp.zeros(out_ref.shape[1:], out_ref.dtype)
    for i, copy in enumerate(copies):
        copy.wait()
        for p in range(parts):
            for s in range(held):
                h = p * held + s
                out_ref[p * slots + s, i] = bufs[i][:, h * HEAD_DIM : (h + 1) * HEAD_DIM]


def pack(arrays, parts, held, n_dev):
    local, feat = arrays[0].shape
    count = len(arrays)
    return pl.pallas_call(
        functools.partial(pack_kernel, parts, held),
        out_shape=jax.ShapeDtypeStruct((n_dev, count, local, HEAD_DIM), jnp.bfloat16),
        in_specs=[pl.BlockSpec(memory_space=pl.ANY)] * count,
        out_specs=pl.BlockSpec(memory_space=pltpu.VMEM),
        scratch_shapes=[pltpu.VMEM((local, feat), jnp.bfloat16)] * count + [pltpu.SemaphoreType.DMA((count,))],
        compiler_params=pltpu.CompilerParams(vmem_limit_bytes=60 * 1024 * 1024),
        cost_estimate=pl.CostEstimate(flops=0, bytes_accessed=count * local * feat * 5, transcendentals=0),
        name="pack",
    )(*arrays)


def unpack_kernel(parts, held, in_ref, out_ref):
    slots = in_ref.shape[0] // parts
    for p in range(parts):
        for s in range(held):
            h = p * held + s
            out_ref[:, h * HEAD_DIM : (h + 1) * HEAD_DIM] = in_ref[p * slots + s]


def attention_kernel(block, counts_ref, plan_ref, mask_ref, place_ref, got_ref, gate_ref, out_ref, bias_ref):
    n_dev, _, local, _ = got_ref.shape
    per_group = n_dev // GROUPS
    group_tok = per_group * local
    rows = block * local
    factor = math.log2(math.e) / math.sqrt(HEAD_DIM)
    head = place_ref[0]
    busy = place_ref[1]

    @pl.when(busy == 1)
    def _():
        gates = gate_ref[:, pl.ds(pl.multiple_of(head * HEAD_DIM, HEAD_DIM), HEAD_DIM)]
        level = lax.broadcasted_iota(jnp.int32, (LEVELS, HEAD_DIM), 0)
        place = lax.broadcasted_iota(jnp.int32, (group_tok, HEAD_DIM), 0)
        for d in range(GROUPS):
            bias_ref[d] = jnp.where(place < counts_ref[d], 0.0, -1e30).astype(jnp.bfloat16)
        lane = lax.broadcasted_iota(jnp.int32, (rows, HEAD_DIM), 1)
        one = jnp.where(lane == 0, 1.0, 0.0).astype(jnp.bfloat16)
        ones = jnp.ones((group_tok, HEAD_DIM), jnp.bfloat16)

        def group_rows(c, seen):
            gate = jnp.sum(jnp.where(level == plan_ref[c], gates, jnp.float32(0.0)), axis=0, keepdims=True)

            @pl.loop(0, per_group // block)
            def _(step):
                first = c * per_group + step * block
                q = jnp.concatenate([got_ref[pl.ds(first, block), 0].reshape(rows, HEAD_DIM), one], axis=1)
                scores = []
                for d in seen:
                    k = got_ref[d * per_group : (d + 1) * per_group, 1].reshape(group_tok, HEAD_DIM)
                    scores.append(
                        lax.dot_general(
                            q,
                            jnp.concatenate([k, bias_ref[d]], axis=1),
                            (((1,), (1,)), ((), ())),
                            preferred_element_type=jnp.float32,
                        )
                    )
                top = functools.reduce(jnp.maximum, [jnp.max(s, axis=1, keepdims=True) for s in scores])
                mixed = jnp.zeros((rows, 2 * HEAD_DIM), jnp.float32)
                for d, s in zip(seen, scores):
                    weights = jnp.exp2(s * factor - top * factor).astype(jnp.bfloat16)
                    v = got_ref[d * per_group : (d + 1) * per_group, 2].reshape(group_tok, HEAD_DIM)
                    mixed += jnp.dot(
                        weights, jnp.concatenate([v, ones], axis=1), preferred_element_type=jnp.float32
                    )
                position = step * rows + lax.broadcasted_iota(jnp.int32, (rows, 1), 0)
                mixed = mixed[:, :HEAD_DIM] / mixed[:, HEAD_DIM:] * gate
                mixed = jnp.where(position < counts_ref[c], mixed, jnp.float32(0.0))
                out_ref[pl.ds(first, block)] = mixed.astype(jnp.bfloat16).reshape(block, local, HEAD_DIM)

        for c in range(GROUPS):
            pattern = sum((mask_ref[c, d] * 2**d for d in range(c)), jnp.int32(0))
            for bits in range(2**c):
                seen = [d for d in range(c) if bits >> d & 1] + [c]
                pl.when(pattern == bits)(functools.partial(group_rows, c, seen))

    @pl.when(busy == 0)
    def _():
        out_ref[...] = jnp.zeros_like(out_ref)


def head_each(queries, keys, values, counts, plan, group_mask, gate_table):
    axes = ("seq", "head")
    n_dev = lax.axis_size("seq") * lax.axis_size("head")
    local, feat = queries.shape
    heads = feat // HEAD_DIM
    parts = math.gcd(heads, n_dev)
    held, slots = heads // parts, n_dev // parts
    index = lax.axis_index("seq") * lax.axis_size("head") + lax.axis_index("head")
    lane = index % slots
    busy = (lane < held).astype(jnp.int32)
    head = jnp.minimum(index // slots * held + lane, heads - 1)
    place = jnp.stack([head, busy]).astype(jnp.int32)
    smem = pl.BlockSpec(memory_space=pltpu.SMEM)
    vmem = pl.BlockSpec(memory_space=pltpu.VMEM)

    sent = pack((queries, keys, values), parts, held, n_dev)
    got = lax.all_to_all(sent, axes, split_axis=0, concat_axis=0, tiled=True)
    result = pl.pallas_call(
        functools.partial(attention_kernel, max(1, 256 // local)),
        out_shape=jax.ShapeDtypeStruct((n_dev, local, HEAD_DIM), jnp.bfloat16),
        in_specs=[smem, smem, smem, smem, vmem, vmem],
        out_specs=vmem,
        scratch_shapes=[pltpu.VMEM((GROUPS, n_dev * local // GROUPS, HEAD_DIM), jnp.bfloat16)],
        compiler_params=pltpu.CompilerParams(vmem_limit_bytes=40 * 1024 * 1024),
        name="attention",
    )(counts, plan, group_mask, place, got, gate_table)
    back = lax.all_to_all(result, axes, split_axis=0, concat_axis=0, tiled=True)
    return pl.pallas_call(
        functools.partial(unpack_kernel, parts, held),
        out_shape=jax.ShapeDtypeStruct((local, feat), jnp.bfloat16),
        in_specs=[vmem],
        out_specs=vmem,
        compiler_params=pltpu.CompilerParams(vmem_limit_bytes=16 * 1024 * 1024),
        name="unpack",
    )(back)


def on_device(queries, keys, values, counts, plan, group_mask, gate_table):
    n_dev = lax.axis_size("seq") * lax.axis_size("head")
    heads = queries.shape[1] // HEAD_DIM
    plan_of = head_each if heads <= n_dev <= 2 * heads else gathered
    return plan_of(queries, keys, values, counts, plan, group_mask, gate_table)


def solution(mesh):
    in_specs = (
        P(("seq", "head"), None),
        P(("seq", "head"), None),
        P(("seq", "head"), None),
        P(),
        P(),
        P(),
        P(),
    )
    out_specs = P(("seq", "head"), None)
    return jax.shard_map(
        on_device, mesh=mesh, in_specs=in_specs, out_specs=out_specs, check_vma=False
    )
```

```python
import functools
import math

import jax
import jax.numpy as jnp
from jax import lax
from jax.experimental import pallas as pl
from jax.experimental.pallas import tpu as pltpu
from jax.sharding import PartitionSpec as P

HEAD_DIM = 128
GROUPS = 4
LEVELS = 8


def lookup(table, index):
    hits = index[:, None] == jnp.arange(table.shape[0], dtype=jnp.int32)[None, :]
    return jnp.sum(jnp.where(hits, table[None, :], 0), axis=1)


def attend(
    work_q, k_local, v_local, row_group, row_pos, counts, plan, group_mask, gate_slice, group_tok
):
    rows = work_q.shape[0]
    width = work_q.shape[1]
    heads_here = width // HEAD_DIM
    scale = 1.0 / math.sqrt(HEAD_DIM)
    q_three = work_q.reshape(rows, heads_here, HEAD_DIM)
    row_onehot = (row_group[:, None] == jnp.arange(GROUPS, dtype=jnp.int32)[None, :]).astype(
        jnp.float32
    )
    mask_rows = jnp.dot(row_onehot, group_mask.astype(jnp.float32))
    k_piece = lax.all_gather(k_local, "seq", axis=0, tiled=True)
    v_piece = lax.all_gather(v_local, "seq", axis=0, tiled=True)
    count = k_piece.shape[0]
    index = jnp.arange(count, dtype=jnp.int32)
    k_group = index // group_tok
    k_pos = index % group_tok
    k_onehot = (k_group[:, None] == jnp.arange(GROUPS, dtype=jnp.int32)[None, :]).astype(
        jnp.float32
    )
    k_valid = k_pos < lookup(counts, k_group)
    allowed = (jnp.dot(mask_rows, k_onehot.T) > 0.5) & k_valid[None, :]
    running = jnp.full((heads_here, rows), -1e30, jnp.float32)
    k_three = k_piece.reshape(count, heads_here, HEAD_DIM)
    v_three = v_piece.reshape(count, heads_here, HEAD_DIM)
    scores = (
        jnp.einsum("qhd,khd->hqk", q_three, k_three, preferred_element_type=jnp.float32) * scale
    )
    scores = jnp.where(allowed[None], scores, jnp.float32(-1e30))
    newest = jnp.maximum(running, jnp.max(scores, axis=2))
    weights = jnp.exp(scores - newest[:, :, None]) * allowed[None].astype(jnp.float32)
    total = jnp.sum(weights, axis=2)
    rounded = weights.astype(jnp.bfloat16)
    accum = jnp.einsum("hqk,khd->hqd", rounded, v_three, preferred_element_type=jnp.float32)
    running, total, accum = (newest, total, accum)
    mixed = accum / total[:, :, None]
    mixed = jnp.transpose(mixed, (1, 0, 2)).reshape(rows, width)
    level_rows = lookup(plan, row_group)
    level_hits = level_rows[:, None] == jnp.arange(LEVELS, dtype=jnp.int32)[None, :]
    gates = jnp.sum(
        jnp.where(level_hits[:, :, None], gate_slice[None, :, :], jnp.float32(0.0)), axis=1
    )
    live = row_pos < lookup(counts, row_group)
    return jnp.where(live[:, None], mixed * gates, jnp.float32(0.0)).astype(jnp.bfloat16)


def gathered(queries, keys, values, counts, plan, group_mask, gate_table):
    n_seq = lax.axis_size("seq")
    n_head = lax.axis_size("head")
    per_group = n_seq // GROUPS
    tok_dev = queries.shape[0] * n_head
    group_tok = tok_dev * per_group
    q_local, k_local, v_local = (
        lax.all_to_all(queries, "head", split_axis=1, concat_axis=0, tiled=True),
        lax.all_to_all(keys, "head", split_axis=1, concat_axis=0, tiled=True),
        lax.all_to_all(values, "head", split_axis=1, concat_axis=0, tiled=True),
    )
    width = q_local.shape[1]
    seq_index = lax.axis_index("seq")
    own_group = seq_index // per_group
    positions = seq_index % per_group * tok_dev + jnp.arange(tok_dev, dtype=jnp.int32)
    gate_slice = lax.dynamic_slice_in_dim(gate_table, lax.axis_index("head") * width, width, 1)
    row_group = jnp.full((tok_dev,), own_group, jnp.int32)
    result = attend(
        q_local,
        k_local,
        v_local,
        row_group,
        positions,
        counts,
        plan,
        group_mask,
        gate_slice,
        group_tok,
    )
    return lax.all_to_all(result, "head", split_axis=0, concat_axis=1, tiled=True)


def pack_kernel(parts, held, *refs):
    count = (len(refs) - 2) // 2
    in_refs, out_ref, bufs, sems = refs[:count], refs[count], refs[count + 1 : -1], refs[-1]
    slots = out_ref.shape[0] // parts
    copies = [pltpu.make_async_copy(in_refs[i], bufs[i], sems.at[i]) for i in range(count)]
    for copy in copies:
        copy.start()
    for s in range(held, slots):
        for p in range(parts):
            out_ref[p * slots + s] = jnp.zeros(out_ref.shape[1:], out_ref.dtype)
    for i, copy in enumerate(copies):
        copy.wait()
        for p in range(parts):
            for s in range(held):
                h = p * held + s
                out_ref[p * slots + s, i] = bufs[i][:, h * HEAD_DIM : (h + 1) * HEAD_DIM]


def pack(arrays, parts, held, n_dev):
    local, feat = arrays[0].shape
    count = len(arrays)
    return pl.pallas_call(
        functools.partial(pack_kernel, parts, held),
        out_shape=jax.ShapeDtypeStruct((n_dev, count, local, HEAD_DIM), jnp.bfloat16),
        in_specs=[pl.BlockSpec(memory_space=pl.ANY)] * count,
        out_specs=pl.BlockSpec(memory_space=pltpu.VMEM),
        scratch_shapes=[pltpu.VMEM((local, feat), jnp.bfloat16)] * count + [pltpu.SemaphoreType.DMA((count,))],
        compiler_params=pltpu.CompilerParams(vmem_limit_bytes=60 * 1024 * 1024),
        cost_estimate=pl.CostEstimate(flops=0, bytes_accessed=count * local * feat * 5, transcendentals=0),
        name="pack",
    )(*arrays)


def unpack_kernel(parts, held, in_ref, out_ref):
    slots = in_ref.shape[0] // parts
    for p in range(parts):
        for s in range(held):
            h = p * held + s
            out_ref[:, h * HEAD_DIM : (h + 1) * HEAD_DIM] = in_ref[p * slots + s]


def attention_kernel(
    counts_ref, plan_ref, mask_ref, place_ref, got_ref, gate_ref, out_ref, bias_ref, score_ref, top_ref, mixed_ref
):
    n_dev, _, local, _ = got_ref.shape
    per_group = n_dev // GROUPS
    rows = per_group * local
    factor = math.log2(math.e) / math.sqrt(HEAD_DIM)
    head = place_ref[0]
    busy = place_ref[1]

    @pl.when(busy == 1)
    def _():
        gates = gate_ref[:, pl.ds(pl.multiple_of(head * HEAD_DIM, HEAD_DIM), HEAD_DIM)]
        level = lax.broadcasted_iota(jnp.int32, (LEVELS, HEAD_DIM), 0)
        place = lax.broadcasted_iota(jnp.int32, (rows, HEAD_DIM), 0)
        lane = lax.broadcasted_iota(jnp.int32, (rows, HEAD_DIM), 1)
        one = jnp.where(lane == 0, 1.0, 0.0).astype(jnp.bfloat16)
        ones = jnp.ones((rows, HEAD_DIM), jnp.bfloat16)

        def part(group, kind):
            return got_ref[pl.ds(group * per_group, per_group), kind].reshape(rows, HEAD_DIM)

        @pl.loop(0, GROUPS)
        def _(c):
            bias_ref[c] = jnp.where(place < counts_ref[c], 0.0, -1e30).astype(jnp.bfloat16)
            top_ref[...] = jnp.full(top_ref.shape, -1e30, jnp.float32)
            mixed_ref[...] = jnp.zeros(mixed_ref.shape, jnp.float32)

            @pl.loop(0, c + 1)
            def _(d):
                @pl.when(mask_ref[c, d] == 1)
                def _():
                    scores = lax.dot_general(
                        jnp.concatenate([part(c, 0), one], axis=1),
                        jnp.concatenate([part(d, 1), bias_ref[d]], axis=1),
                        (((1,), (1,)), ((), ())),
                        preferred_element_type=jnp.float32,
                    )
                    score_ref[d] = scores
                    pieces = [scores[:, i : i + HEAD_DIM] for i in range(0, rows, HEAD_DIM)]
                    top_ref[...] = functools.reduce(jnp.maximum, pieces, top_ref[...])

            top = jnp.max(top_ref[...], axis=1, keepdims=True) * factor
            top_ref[...] = jnp.broadcast_to(top, top_ref.shape)

            @pl.loop(0, c + 1)
            def _(d):
                @pl.when(mask_ref[c, d] == 1)
                def _():
                    top = jnp.concatenate([top_ref[...]] * (rows // HEAD_DIM), axis=1)
                    weights = jnp.exp2(score_ref[d] * factor - top).astype(jnp.bfloat16)
                    mixed_ref[...] += jnp.dot(
                        weights, jnp.concatenate([part(d, 2), ones], axis=1), preferred_element_type=jnp.float32
                    )

            gate = jnp.sum(jnp.where(level == plan_ref[c], gates, jnp.float32(0.0)), axis=0, keepdims=True)
            mixed = mixed_ref[:, :HEAD_DIM] / mixed_ref[:, HEAD_DIM:] * gate
            mixed = jnp.where(place < counts_ref[c], mixed, jnp.float32(0.0))
            out_ref[pl.ds(c * per_group, per_group)] = mixed.astype(jnp.bfloat16).reshape(
                per_group, local, HEAD_DIM
            )

    @pl.when(busy == 0)
    def _():
        out_ref[...] = jnp.zeros_like(out_ref)


def head_each(queries, keys, values, counts, plan, group_mask, gate_table):
    axes = ("seq", "head")
    n_dev = lax.axis_size("seq") * lax.axis_size("head")
    local, feat = queries.shape
    heads = feat // HEAD_DIM
    parts = math.gcd(heads, n_dev)
    held, slots = heads // parts, n_dev // parts
    index = lax.axis_index("seq") * lax.axis_size("head") + lax.axis_index("head")
    lane = index % slots
    busy = (lane < held).astype(jnp.int32)
    head = jnp.minimum(index // slots * held + lane, heads - 1)
    place = jnp.stack([head, busy]).astype(jnp.int32)
    smem = pl.BlockSpec(memory_space=pltpu.SMEM)
    vmem = pl.BlockSpec(memory_space=pltpu.VMEM)

    sent = pack((queries, keys, values), parts, held, n_dev)
    got = lax.all_to_all(sent, axes, split_axis=0, concat_axis=0, tiled=True)
    rows = n_dev * local // GROUPS
    result = pl.pallas_call(
        attention_kernel,
        out_shape=jax.ShapeDtypeStruct((n_dev, local, HEAD_DIM), jnp.bfloat16),
        in_specs=[smem, smem, smem, smem, vmem, vmem],
        out_specs=vmem,
        scratch_shapes=[
            pltpu.VMEM((GROUPS, rows, HEAD_DIM), jnp.bfloat16),
            pltpu.VMEM((GROUPS, rows, rows), jnp.float32),
            pltpu.VMEM((rows, HEAD_DIM), jnp.float32),
            pltpu.VMEM((rows, 2 * HEAD_DIM), jnp.float32),
        ],
        compiler_params=pltpu.CompilerParams(vmem_limit_bytes=40 * 1024 * 1024),
        name="attention",
    )(counts, plan, group_mask, place, got, gate_table)
    back = lax.all_to_all(result, axes, split_axis=0, concat_axis=0, tiled=True)
    return pl.pallas_call(
        functools.partial(unpack_kernel, parts, held),
        out_shape=jax.ShapeDtypeStruct((local, feat), jnp.bfloat16),
        in_specs=[vmem],
        out_specs=vmem,
        compiler_params=pltpu.CompilerParams(vmem_limit_bytes=16 * 1024 * 1024),
        name="unpack",
    )(back)


def on_device(queries, keys, values, counts, plan, group_mask, gate_table):
    n_dev = lax.axis_size("seq") * lax.axis_size("head")
    heads = queries.shape[1] // HEAD_DIM
    plan_of = head_each if heads <= n_dev <= 2 * heads else gathered
    return plan_of(queries, keys, values, counts, plan, group_mask, gate_table)


def solution(mesh):
    in_specs = (
        P(("seq", "head"), None),
        P(("seq", "head"), None),
        P(("seq", "head"), None),
        P(),
        P(),
        P(),
        P(),
    )
    out_specs = P(("seq", "head"), None)
    return jax.shard_map(
        on_device, mesh=mesh, in_specs=in_specs, out_specs=out_specs, check_vma=False
    )
```

```python
import functools
import math

import jax
import jax.numpy as jnp
from jax import lax
from jax.experimental import pallas as pl
from jax.experimental.pallas import tpu as pltpu
from jax.sharding import PartitionSpec as P

HEAD_DIM = 128
GROUPS = 4
LEVELS = 8


def lookup(table, index):
    hits = index[:, None] == jnp.arange(table.shape[0], dtype=jnp.int32)[None, :]
    return jnp.sum(jnp.where(hits, table[None, :], 0), axis=1)


def attend(
    work_q, k_local, v_local, row_group, row_pos, counts, plan, group_mask, gate_slice, group_tok
):
    rows = work_q.shape[0]
    width = work_q.shape[1]
    heads_here = width // HEAD_DIM
    scale = 1.0 / math.sqrt(HEAD_DIM)
    q_three = work_q.reshape(rows, heads_here, HEAD_DIM)
    row_onehot = (row_group[:, None] == jnp.arange(GROUPS, dtype=jnp.int32)[None, :]).astype(
        jnp.float32
    )
    mask_rows = jnp.dot(row_onehot, group_mask.astype(jnp.float32))
    k_piece = lax.all_gather(k_local, "seq", axis=0, tiled=True)
    v_piece = lax.all_gather(v_local, "seq", axis=0, tiled=True)
    count = k_piece.shape[0]
    index = jnp.arange(count, dtype=jnp.int32)
    k_group = index // group_tok
    k_pos = index % group_tok
    k_onehot = (k_group[:, None] == jnp.arange(GROUPS, dtype=jnp.int32)[None, :]).astype(
        jnp.float32
    )
    k_valid = k_pos < lookup(counts, k_group)
    allowed = (jnp.dot(mask_rows, k_onehot.T) > 0.5) & k_valid[None, :]
    running = jnp.full((heads_here, rows), -1e30, jnp.float32)
    k_three = k_piece.reshape(count, heads_here, HEAD_DIM)
    v_three = v_piece.reshape(count, heads_here, HEAD_DIM)
    scores = (
        jnp.einsum("qhd,khd->hqk", q_three, k_three, preferred_element_type=jnp.float32) * scale
    )
    scores = jnp.where(allowed[None], scores, jnp.float32(-1e30))
    newest = jnp.maximum(running, jnp.max(scores, axis=2))
    weights = jnp.exp(scores - newest[:, :, None]) * allowed[None].astype(jnp.float32)
    total = jnp.sum(weights, axis=2)
    rounded = weights.astype(jnp.bfloat16)
    accum = jnp.einsum("hqk,khd->hqd", rounded, v_three, preferred_element_type=jnp.float32)
    running, total, accum = (newest, total, accum)
    mixed = accum / total[:, :, None]
    mixed = jnp.transpose(mixed, (1, 0, 2)).reshape(rows, width)
    level_rows = lookup(plan, row_group)
    level_hits = level_rows[:, None] == jnp.arange(LEVELS, dtype=jnp.int32)[None, :]
    gates = jnp.sum(
        jnp.where(level_hits[:, :, None], gate_slice[None, :, :], jnp.float32(0.0)), axis=1
    )
    live = row_pos < lookup(counts, row_group)
    return jnp.where(live[:, None], mixed * gates, jnp.float32(0.0)).astype(jnp.bfloat16)


def gathered(queries, keys, values, counts, plan, group_mask, gate_table):
    n_seq = lax.axis_size("seq")
    n_head = lax.axis_size("head")
    per_group = n_seq // GROUPS
    tok_dev = queries.shape[0] * n_head
    group_tok = tok_dev * per_group
    q_local, k_local, v_local = (
        lax.all_to_all(queries, "head", split_axis=1, concat_axis=0, tiled=True),
        lax.all_to_all(keys, "head", split_axis=1, concat_axis=0, tiled=True),
        lax.all_to_all(values, "head", split_axis=1, concat_axis=0, tiled=True),
    )
    width = q_local.shape[1]
    seq_index = lax.axis_index("seq")
    own_group = seq_index // per_group
    positions = seq_index % per_group * tok_dev + jnp.arange(tok_dev, dtype=jnp.int32)
    gate_slice = lax.dynamic_slice_in_dim(gate_table, lax.axis_index("head") * width, width, 1)
    row_group = jnp.full((tok_dev,), own_group, jnp.int32)
    result = attend(
        q_local,
        k_local,
        v_local,
        row_group,
        positions,
        counts,
        plan,
        group_mask,
        gate_slice,
        group_tok,
    )
    return lax.all_to_all(result, "head", split_axis=0, concat_axis=1, tiled=True)


def pack_kernel(parts, held, *refs):
    count = (len(refs) - 2) // 2
    in_refs, out_ref, bufs, sems = refs[:count], refs[count], refs[count + 1 : -1], refs[-1]
    slots = out_ref.shape[0] // parts
    copies = [pltpu.make_async_copy(in_refs[i], bufs[i], sems.at[i]) for i in range(count)]
    for copy in copies:
        copy.start()
    for s in range(held, slots):
        for p in range(parts):
            out_ref[p * slots + s] = jnp.zeros(out_ref.shape[1:], out_ref.dtype)
    for i, copy in enumerate(copies):
        copy.wait()
        for p in range(parts):
            for s in range(held):
                h = p * held + s
                out_ref[p * slots + s, i] = bufs[i][:, h * HEAD_DIM : (h + 1) * HEAD_DIM]


def pack(arrays, parts, held, n_dev):
    local, feat = arrays[0].shape
    count = len(arrays)
    return pl.pallas_call(
        functools.partial(pack_kernel, parts, held),
        out_shape=jax.ShapeDtypeStruct((n_dev, count, local, HEAD_DIM), jnp.bfloat16),
        in_specs=[pl.BlockSpec(memory_space=pltpu.HBM)] * count,
        out_specs=pl.BlockSpec(memory_space=pltpu.VMEM),
        scratch_shapes=[pltpu.VMEM((local, feat), jnp.bfloat16)] * count + [pltpu.SemaphoreType.DMA((count,))],
        compiler_params=pltpu.CompilerParams(vmem_limit_bytes=16 * 1024 * 1024),
        cost_estimate=pl.CostEstimate(flops=0, bytes_accessed=count * local * feat * 5, transcendentals=0),
        name="pack",
    )(*arrays)


def unpack_kernel(parts, held, in_ref, out_ref):
    slots = in_ref.shape[0] // parts
    for p in range(parts):
        for s in range(held):
            h = p * held + s
            out_ref[:, h * HEAD_DIM : (h + 1) * HEAD_DIM] = in_ref[p * slots + s]


def attention_kernel(
    counts_ref, plan_ref, mask_ref, place_ref, got_ref, gate_ref, out_ref, bias_ref, top_ref, mixed_ref
):
    n_dev, _, local, _ = got_ref.shape
    per_group = n_dev // GROUPS
    rows = per_group * local
    factor = math.log2(math.e) / math.sqrt(HEAD_DIM)
    head = place_ref[0]
    busy = place_ref[1]

    @pl.when(busy == 1)
    def _():
        gates = gate_ref[:, pl.ds(pl.multiple_of(head * HEAD_DIM, HEAD_DIM), HEAD_DIM)]
        level = lax.broadcasted_iota(jnp.int32, (LEVELS, HEAD_DIM), 0)
        place = lax.broadcasted_iota(jnp.int32, (rows, HEAD_DIM), 0)
        lane = lax.broadcasted_iota(jnp.int32, (rows, HEAD_DIM), 1)
        one = jnp.where(lane == 0, 1.0, 0.0).astype(jnp.bfloat16)
        ones = jnp.ones((rows, HEAD_DIM), jnp.bfloat16)

        def part(group, kind):
            return got_ref[pl.ds(group * per_group, per_group), kind].reshape(rows, HEAD_DIM)

        @pl.loop(0, GROUPS)
        def _(c):
            bias_ref[c] = jnp.where(place < counts_ref[c], 0.0, -1e30).astype(jnp.bfloat16)
            top_ref[...] = jnp.full(top_ref.shape, -1e30, jnp.float32)
            mixed_ref[...] = jnp.zeros(mixed_ref.shape, jnp.float32)

            @pl.loop(0, c + 1)
            def _(d):
                @pl.when(mask_ref[c, d] == 1)
                def _():
                    k = jnp.concatenate([part(d, 1), bias_ref[d]], axis=1)
                    v = jnp.concatenate([part(d, 2), ones], axis=1)
                    half = rows // 2
                    for start in (0, half):
                        own = slice(start, start + half)
                        scores = lax.dot_general(
                            jnp.concatenate([part(c, 0)[own], one[own]], axis=1),
                            k,
                            (((1,), (1,)), ((), ())),
                            preferred_element_type=jnp.float32,
                        )
                        old = top_ref[own]
                        top = jnp.maximum(old, jnp.max(scores, axis=1, keepdims=True))
                        top_ref[own] = top
                        shift = jnp.concatenate([top * factor] * (rows // HEAD_DIM), axis=1)
                        weights = jnp.exp2(scores * factor - shift).astype(jnp.bfloat16)
                        fade = jnp.exp2((old - top) * factor)
                        mixed_ref[own] = mixed_ref[own] * jnp.concatenate([fade, fade], axis=1) + jnp.dot(
                            weights, v, preferred_element_type=jnp.float32
                        )

            gate = jnp.sum(jnp.where(level == plan_ref[c], gates, jnp.float32(0.0)), axis=0, keepdims=True)
            mixed = mixed_ref[:, :HEAD_DIM] / mixed_ref[:, HEAD_DIM:] * gate
            mixed = jnp.where(place < counts_ref[c], mixed, jnp.float32(0.0))
            out_ref[pl.ds(c * per_group, per_group)] = mixed.astype(jnp.bfloat16).reshape(
                per_group, local, HEAD_DIM
            )

    @pl.when(busy == 0)
    def _():
        out_ref[...] = jnp.zeros_like(out_ref)


def head_each(queries, keys, values, counts, plan, group_mask, gate_table):
    axes = ("seq", "head")
    n_dev = lax.axis_size("seq") * lax.axis_size("head")
    local, feat = queries.shape
    heads = feat // HEAD_DIM
    parts = math.gcd(heads, n_dev)
    held, slots = heads // parts, n_dev // parts
    index = lax.axis_index("seq") * lax.axis_size("head") + lax.axis_index("head")
    lane = index % slots
    busy = (lane < held).astype(jnp.int32)
    head = jnp.minimum(index // slots * held + lane, heads - 1)
    place = jnp.stack([head, busy]).astype(jnp.int32)
    smem = pl.BlockSpec(memory_space=pltpu.SMEM)
    vmem = pl.BlockSpec(memory_space=pltpu.VMEM)

    sent = pack((queries, keys, values), parts, held, n_dev)
    got = lax.all_to_all(sent, axes, split_axis=0, concat_axis=0, tiled=True)
    rows = n_dev * local // GROUPS
    result = pl.pallas_call(
        attention_kernel,
        out_shape=jax.ShapeDtypeStruct((n_dev, local, HEAD_DIM), jnp.bfloat16),
        in_specs=[smem, smem, smem, smem, vmem, vmem],
        out_specs=vmem,
        scratch_shapes=[
            pltpu.VMEM((GROUPS, rows, HEAD_DIM), jnp.bfloat16),
            pltpu.VMEM((rows, HEAD_DIM), jnp.float32),
            pltpu.VMEM((rows, 2 * HEAD_DIM), jnp.float32),
        ],
        compiler_params=pltpu.CompilerParams(vmem_limit_bytes=40 * 1024 * 1024),
        name="attention",
    )(counts, plan, group_mask, place, got, gate_table)
    back = lax.all_to_all(result, axes, split_axis=0, concat_axis=0, tiled=True)
    return pl.pallas_call(
        functools.partial(unpack_kernel, parts, held),
        out_shape=jax.ShapeDtypeStruct((local, feat), jnp.bfloat16),
        in_specs=[vmem],
        out_specs=vmem,
        compiler_params=pltpu.CompilerParams(vmem_limit_bytes=16 * 1024 * 1024),
        name="unpack",
    )(back)


def on_device(queries, keys, values, counts, plan, group_mask, gate_table):
    n_dev = lax.axis_size("seq") * lax.axis_size("head")
    heads = queries.shape[1] // HEAD_DIM
    plan_of = head_each if heads <= n_dev <= 2 * heads else gathered
    return plan_of(queries, keys, values, counts, plan, group_mask, gate_table)


def solution(mesh):
    in_specs = (
        P(("seq", "head"), None),
        P(("seq", "head"), None),
        P(("seq", "head"), None),
        P(),
        P(),
        P(),
        P(),
    )
    out_specs = P(("seq", "head"), None)
    return jax.shard_map(
        on_device, mesh=mesh, in_specs=in_specs, out_specs=out_specs, check_vma=False
    )
```

```python
import functools
import math

import jax
import jax.numpy as jnp
from jax import lax
from jax.experimental import pallas as pl
from jax.experimental.pallas import tpu as pltpu
from jax.sharding import PartitionSpec as P

HEAD_DIM = 128
GROUPS = 4
LEVELS = 8


def lookup(table, index):
    hits = index[:, None] == jnp.arange(table.shape[0], dtype=jnp.int32)[None, :]
    return jnp.sum(jnp.where(hits, table[None, :], 0), axis=1)


def attend(
    work_q, k_local, v_local, row_group, row_pos, counts, plan, group_mask, gate_slice, group_tok
):
    rows = work_q.shape[0]
    width = work_q.shape[1]
    heads_here = width // HEAD_DIM
    scale = 1.0 / math.sqrt(HEAD_DIM)
    q_three = work_q.reshape(rows, heads_here, HEAD_DIM)
    row_onehot = (row_group[:, None] == jnp.arange(GROUPS, dtype=jnp.int32)[None, :]).astype(
        jnp.float32
    )
    mask_rows = jnp.dot(row_onehot, group_mask.astype(jnp.float32))
    k_piece = lax.all_gather(k_local, "seq", axis=0, tiled=True)
    v_piece = lax.all_gather(v_local, "seq", axis=0, tiled=True)
    count = k_piece.shape[0]
    index = jnp.arange(count, dtype=jnp.int32)
    k_group = index // group_tok
    k_pos = index % group_tok
    k_onehot = (k_group[:, None] == jnp.arange(GROUPS, dtype=jnp.int32)[None, :]).astype(
        jnp.float32
    )
    k_valid = k_pos < lookup(counts, k_group)
    allowed = (jnp.dot(mask_rows, k_onehot.T) > 0.5) & k_valid[None, :]
    running = jnp.full((heads_here, rows), -1e30, jnp.float32)
    k_three = k_piece.reshape(count, heads_here, HEAD_DIM)
    v_three = v_piece.reshape(count, heads_here, HEAD_DIM)
    scores = (
        jnp.einsum("qhd,khd->hqk", q_three, k_three, preferred_element_type=jnp.float32) * scale
    )
    scores = jnp.where(allowed[None], scores, jnp.float32(-1e30))
    newest = jnp.maximum(running, jnp.max(scores, axis=2))
    weights = jnp.exp(scores - newest[:, :, None]) * allowed[None].astype(jnp.float32)
    total = jnp.sum(weights, axis=2)
    rounded = weights.astype(jnp.bfloat16)
    accum = jnp.einsum("hqk,khd->hqd", rounded, v_three, preferred_element_type=jnp.float32)
    running, total, accum = (newest, total, accum)
    mixed = accum / total[:, :, None]
    mixed = jnp.transpose(mixed, (1, 0, 2)).reshape(rows, width)
    level_rows = lookup(plan, row_group)
    level_hits = level_rows[:, None] == jnp.arange(LEVELS, dtype=jnp.int32)[None, :]
    gates = jnp.sum(
        jnp.where(level_hits[:, :, None], gate_slice[None, :, :], jnp.float32(0.0)), axis=1
    )
    live = row_pos < lookup(counts, row_group)
    return jnp.where(live[:, None], mixed * gates, jnp.float32(0.0)).astype(jnp.bfloat16)


def gathered(queries, keys, values, counts, plan, group_mask, gate_table):
    n_seq = lax.axis_size("seq")
    n_head = lax.axis_size("head")
    per_group = n_seq // GROUPS
    tok_dev = queries.shape[0] * n_head
    group_tok = tok_dev * per_group
    q_local, k_local, v_local = (
        lax.all_to_all(queries, "head", split_axis=1, concat_axis=0, tiled=True),
        lax.all_to_all(keys, "head", split_axis=1, concat_axis=0, tiled=True),
        lax.all_to_all(values, "head", split_axis=1, concat_axis=0, tiled=True),
    )
    width = q_local.shape[1]
    seq_index = lax.axis_index("seq")
    own_group = seq_index // per_group
    positions = seq_index % per_group * tok_dev + jnp.arange(tok_dev, dtype=jnp.int32)
    gate_slice = lax.dynamic_slice_in_dim(gate_table, lax.axis_index("head") * width, width, 1)
    row_group = jnp.full((tok_dev,), own_group, jnp.int32)
    result = attend(
        q_local,
        k_local,
        v_local,
        row_group,
        positions,
        counts,
        plan,
        group_mask,
        gate_slice,
        group_tok,
    )
    return lax.all_to_all(result, "head", split_axis=0, concat_axis=1, tiled=True)


def pack_kernel(parts, held, q_ref, k_ref, v_ref, out_ref, zero_ref, sem):
    slots = out_ref.shape[0] // parts
    zero_ref[...] = jnp.zeros_like(zero_ref)
    for p in range(parts):
        for s in range(held):
            h = p * held + s
            for i, ref in enumerate((q_ref, k_ref, v_ref)):
                pltpu.make_async_copy(
                    ref.at[:, h * HEAD_DIM : (h + 1) * HEAD_DIM], out_ref.at[p * slots + s, i], sem
                ).start()
        for s in range(held, slots):
            pltpu.make_async_copy(zero_ref, out_ref.at[p * slots + s], sem).start()
    pltpu.make_async_copy(out_ref, out_ref, sem).wait()


def pack(arrays, parts, held, n_dev):
    local, _ = arrays[0].shape
    count = len(arrays)
    return pl.pallas_call(
        functools.partial(pack_kernel, parts, held),
        out_shape=jax.ShapeDtypeStruct((n_dev, count, local, HEAD_DIM), jnp.bfloat16),
        in_specs=[pl.BlockSpec(memory_space=pl.ANY)] * count,
        out_specs=pl.BlockSpec(memory_space=pl.ANY),
        scratch_shapes=[pltpu.VMEM((count, local, HEAD_DIM), jnp.bfloat16), pltpu.SemaphoreType.DMA],
        compiler_params=pltpu.CompilerParams(vmem_limit_bytes=60 * 1024 * 1024),
        name="pack",
    )(*arrays)


def unpack_kernel(parts, held, in_ref, out_ref, sem):
    slots = in_ref.shape[0] // parts
    for p in range(parts):
        for s in range(held):
            h = p * held + s
            pltpu.make_async_copy(
                in_ref.at[p * slots + s], out_ref.at[:, h * HEAD_DIM : (h + 1) * HEAD_DIM], sem
            ).start()
    pltpu.make_async_copy(out_ref, out_ref, sem).wait()


def attention_kernel(
    counts_ref, plan_ref, mask_ref, place_ref, got_ref, gate_ref, out_ref, bias_ref, score_ref, top_ref, mixed_ref
):
    n_dev, _, local, _ = got_ref.shape
    per_group = n_dev // GROUPS
    rows = per_group * local
    factor = math.log2(math.e) / math.sqrt(HEAD_DIM)
    head = place_ref[0]
    busy = place_ref[1]

    @pl.when(busy == 1)
    def _():
        gates = gate_ref[:, pl.ds(pl.multiple_of(head * HEAD_DIM, HEAD_DIM), HEAD_DIM)]
        level = lax.broadcasted_iota(jnp.int32, (LEVELS, HEAD_DIM), 0)
        place = lax.broadcasted_iota(jnp.int32, (rows, HEAD_DIM), 0)
        lane = lax.broadcasted_iota(jnp.int32, (rows, HEAD_DIM), 1)
        one = jnp.where(lane == 0, 1.0, 0.0).astype(jnp.bfloat16)
        ones = jnp.ones((rows, HEAD_DIM), jnp.bfloat16)

        def part(group, kind):
            return got_ref[pl.ds(group * per_group, per_group), kind].reshape(rows, HEAD_DIM)

        @pl.loop(0, GROUPS)
        def _(c):
            bias_ref[c] = jnp.where(place < counts_ref[c], 0.0, -1e30).astype(jnp.bfloat16)
            top_ref[...] = jnp.full(top_ref.shape, -1e30, jnp.float32)
            mixed_ref[...] = jnp.zeros(mixed_ref.shape, jnp.float32)

            @pl.loop(0, c + 1)
            def _(d):
                @pl.when(mask_ref[c, d] == 1)
                def _():
                    scores = lax.dot_general(
                        jnp.concatenate([part(c, 0), one], axis=1),
                        jnp.concatenate([part(d, 1), bias_ref[d]], axis=1),
                        (((1,), (1,)), ((), ())),
                        preferred_element_type=jnp.float32,
                    )
                    score_ref[d] = scores
                    pieces = [scores[:, i : i + HEAD_DIM] for i in range(0, rows, HEAD_DIM)]
                    top_ref[...] = functools.reduce(jnp.maximum, pieces, top_ref[...])

            top = jnp.max(top_ref[...], axis=1, keepdims=True) * factor
            top_ref[...] = jnp.broadcast_to(top, top_ref.shape)

            @pl.loop(0, c + 1)
            def _(d):
                @pl.when(mask_ref[c, d] == 1)
                def _():
                    top = jnp.concatenate([top_ref[...]] * (rows // HEAD_DIM), axis=1)
                    weights = jnp.exp2(score_ref[d] * factor - top).astype(jnp.bfloat16)
                    mixed_ref[...] += jnp.dot(
                        weights, jnp.concatenate([part(d, 2), ones], axis=1), preferred_element_type=jnp.float32
                    )

            gate = jnp.sum(jnp.where(level == plan_ref[c], gates, jnp.float32(0.0)), axis=0, keepdims=True)
            mixed = mixed_ref[:, :HEAD_DIM] / mixed_ref[:, HEAD_DIM:] * gate
            mixed = jnp.where(place < counts_ref[c], mixed, jnp.float32(0.0))
            out_ref[pl.ds(c * per_group, per_group)] = mixed.astype(jnp.bfloat16).reshape(
                per_group, local, HEAD_DIM
            )

    @pl.when(busy == 0)
    def _():
        out_ref[...] = jnp.zeros_like(out_ref)


def head_each(queries, keys, values, counts, plan, group_mask, gate_table):
    axes = ("seq", "head")
    n_dev = lax.axis_size("seq") * lax.axis_size("head")
    local, feat = queries.shape
    heads = feat // HEAD_DIM
    parts = math.gcd(heads, n_dev)
    held, slots = heads // parts, n_dev // parts
    index = lax.axis_index("seq") * lax.axis_size("head") + lax.axis_index("head")
    lane = index % slots
    busy = (lane < held).astype(jnp.int32)
    head = jnp.minimum(index // slots * held + lane, heads - 1)
    place = jnp.stack([head, busy]).astype(jnp.int32)
    smem = pl.BlockSpec(memory_space=pltpu.SMEM)
    vmem = pl.BlockSpec(memory_space=pltpu.VMEM)

    sent = pack((queries, keys, values), parts, held, n_dev)
    got = lax.all_to_all(sent, axes, split_axis=0, concat_axis=0, tiled=True)
    rows = n_dev * local // GROUPS
    result = pl.pallas_call(
        attention_kernel,
        out_shape=jax.ShapeDtypeStruct((n_dev, local, HEAD_DIM), jnp.bfloat16),
        in_specs=[smem, smem, smem, smem, vmem, vmem],
        out_specs=vmem,
        scratch_shapes=[
            pltpu.VMEM((GROUPS, rows, HEAD_DIM), jnp.bfloat16),
            pltpu.VMEM((GROUPS, rows, rows), jnp.float32),
            pltpu.VMEM((rows, HEAD_DIM), jnp.float32),
            pltpu.VMEM((rows, 2 * HEAD_DIM), jnp.float32),
        ],
        compiler_params=pltpu.CompilerParams(vmem_limit_bytes=40 * 1024 * 1024),
        name="attention",
    )(counts, plan, group_mask, place, got, gate_table)
    back = lax.all_to_all(result, axes, split_axis=0, concat_axis=0, tiled=True)
    return pl.pallas_call(
        functools.partial(unpack_kernel, parts, held),
        out_shape=jax.ShapeDtypeStruct((local, feat), jnp.bfloat16),
        in_specs=[vmem],
        out_specs=pl.BlockSpec(memory_space=pl.ANY),
        scratch_shapes=[pltpu.SemaphoreType.DMA],
        compiler_params=pltpu.CompilerParams(vmem_limit_bytes=16 * 1024 * 1024),
        name="unpack",
    )(back)


def on_device(queries, keys, values, counts, plan, group_mask, gate_table):
    n_dev = lax.axis_size("seq") * lax.axis_size("head")
    heads = queries.shape[1] // HEAD_DIM
    plan_of = head_each if heads <= n_dev <= 2 * heads else gathered
    return plan_of(queries, keys, values, counts, plan, group_mask, gate_table)


def solution(mesh):
    in_specs = (
        P(("seq", "head"), None),
        P(("seq", "head"), None),
        P(("seq", "head"), None),
        P(),
        P(),
        P(),
        P(),
    )
    out_specs = P(("seq", "head"), None)
    return jax.shard_map(
        on_device, mesh=mesh, in_specs=in_specs, out_specs=out_specs, check_vma=False
    )
```

```python
import functools
import math

import jax
import jax.numpy as jnp
from jax import lax
from jax.experimental import pallas as pl
from jax.experimental.pallas import tpu as pltpu
from jax.sharding import PartitionSpec as P

HEAD_DIM = 128
GROUPS = 4
LEVELS = 8


def lookup(table, index):
    hits = index[:, None] == jnp.arange(table.shape[0], dtype=jnp.int32)[None, :]
    return jnp.sum(jnp.where(hits, table[None, :], 0), axis=1)


def attend(
    work_q, k_local, v_local, row_group, row_pos, counts, plan, group_mask, gate_slice, group_tok
):
    rows = work_q.shape[0]
    width = work_q.shape[1]
    heads_here = width // HEAD_DIM
    scale = 1.0 / math.sqrt(HEAD_DIM)
    q_three = work_q.reshape(rows, heads_here, HEAD_DIM)
    row_onehot = (row_group[:, None] == jnp.arange(GROUPS, dtype=jnp.int32)[None, :]).astype(
        jnp.float32
    )
    mask_rows = jnp.dot(row_onehot, group_mask.astype(jnp.float32))
    k_piece = lax.all_gather(k_local, "seq", axis=0, tiled=True)
    v_piece = lax.all_gather(v_local, "seq", axis=0, tiled=True)
    count = k_piece.shape[0]
    index = jnp.arange(count, dtype=jnp.int32)
    k_group = index // group_tok
    k_pos = index % group_tok
    k_onehot = (k_group[:, None] == jnp.arange(GROUPS, dtype=jnp.int32)[None, :]).astype(
        jnp.float32
    )
    k_valid = k_pos < lookup(counts, k_group)
    allowed = (jnp.dot(mask_rows, k_onehot.T) > 0.5) & k_valid[None, :]
    running = jnp.full((heads_here, rows), -1e30, jnp.float32)
    k_three = k_piece.reshape(count, heads_here, HEAD_DIM)
    v_three = v_piece.reshape(count, heads_here, HEAD_DIM)
    scores = (
        jnp.einsum("qhd,khd->hqk", q_three, k_three, preferred_element_type=jnp.float32) * scale
    )
    scores = jnp.where(allowed[None], scores, jnp.float32(-1e30))
    newest = jnp.maximum(running, jnp.max(scores, axis=2))
    weights = jnp.exp(scores - newest[:, :, None]) * allowed[None].astype(jnp.float32)
    total = jnp.sum(weights, axis=2)
    rounded = weights.astype(jnp.bfloat16)
    accum = jnp.einsum("hqk,khd->hqd", rounded, v_three, preferred_element_type=jnp.float32)
    running, total, accum = (newest, total, accum)
    mixed = accum / total[:, :, None]
    mixed = jnp.transpose(mixed, (1, 0, 2)).reshape(rows, width)
    level_rows = lookup(plan, row_group)
    level_hits = level_rows[:, None] == jnp.arange(LEVELS, dtype=jnp.int32)[None, :]
    gates = jnp.sum(
        jnp.where(level_hits[:, :, None], gate_slice[None, :, :], jnp.float32(0.0)), axis=1
    )
    live = row_pos < lookup(counts, row_group)
    return jnp.where(live[:, None], mixed * gates, jnp.float32(0.0)).astype(jnp.bfloat16)


def gathered(queries, keys, values, counts, plan, group_mask, gate_table):
    n_seq = lax.axis_size("seq")
    n_head = lax.axis_size("head")
    per_group = n_seq // GROUPS
    tok_dev = queries.shape[0] * n_head
    group_tok = tok_dev * per_group
    q_local, k_local, v_local = (
        lax.all_to_all(queries, "head", split_axis=1, concat_axis=0, tiled=True),
        lax.all_to_all(keys, "head", split_axis=1, concat_axis=0, tiled=True),
        lax.all_to_all(values, "head", split_axis=1, concat_axis=0, tiled=True),
    )
    width = q_local.shape[1]
    seq_index = lax.axis_index("seq")
    own_group = seq_index // per_group
    positions = seq_index % per_group * tok_dev + jnp.arange(tok_dev, dtype=jnp.int32)
    gate_slice = lax.dynamic_slice_in_dim(gate_table, lax.axis_index("head") * width, width, 1)
    row_group = jnp.full((tok_dev,), own_group, jnp.int32)
    result = attend(
        q_local,
        k_local,
        v_local,
        row_group,
        positions,
        counts,
        plan,
        group_mask,
        gate_slice,
        group_tok,
    )
    return lax.all_to_all(result, "head", split_axis=0, concat_axis=1, tiled=True)


def pack_kernel(parts, held, *refs):
    count = (len(refs) - 2) // 2
    in_refs, out_ref, bufs, sems = refs[:count], refs[count], refs[count + 1 : -1], refs[-1]
    slots = out_ref.shape[0] // parts
    copies = [pltpu.make_async_copy(in_refs[i], bufs[i], sems.at[i]) for i in range(count)]
    for copy in copies:
        copy.start()
    for s in range(held, slots):
        for p in range(parts):
            out_ref[p * slots + s] = jnp.zeros(out_ref.shape[1:], out_ref.dtype)
    for i, copy in enumerate(copies):
        copy.wait()
        for p in range(parts):
            for s in range(held):
                h = p * held + s
                out_ref[p * slots + s, i] = bufs[i][:, h * HEAD_DIM : (h + 1) * HEAD_DIM]


def pack(arrays, parts, held, n_dev):
    local, feat = arrays[0].shape
    count = len(arrays)
    return pl.pallas_call(
        functools.partial(pack_kernel, parts, held),
        out_shape=jax.ShapeDtypeStruct((n_dev, count, local, HEAD_DIM), jnp.bfloat16),
        in_specs=[pl.BlockSpec(memory_space=pl.ANY)] * count,
        out_specs=pl.BlockSpec(memory_space=pltpu.VMEM),
        scratch_shapes=[pltpu.VMEM((local, feat), jnp.bfloat16)] * count + [pltpu.SemaphoreType.DMA((count,))],
        compiler_params=pltpu.CompilerParams(vmem_limit_bytes=60 * 1024 * 1024),
        cost_estimate=pl.CostEstimate(flops=0, bytes_accessed=count * local * feat * 5, transcendentals=0),
        name="pack",
    )(*arrays)


def unpack_kernel(parts, held, in_ref, out_ref, sem):
    slots = in_ref.shape[0] // parts
    for p in range(parts):
        for s in range(held):
            h = p * held + s
            pltpu.make_async_copy(
                in_ref.at[p * slots + s], out_ref.at[:, h * HEAD_DIM : (h + 1) * HEAD_DIM], sem
            ).start()
    pltpu.make_async_copy(out_ref, out_ref, sem).wait()


def attention_kernel(
    counts_ref, plan_ref, mask_ref, place_ref, got_ref, gate_ref, out_ref, bias_ref, score_ref, top_ref, mixed_ref
):
    n_dev, _, local, _ = got_ref.shape
    per_group = n_dev // GROUPS
    rows = per_group * local
    factor = 1.0 / math.sqrt(HEAD_DIM)
    head = place_ref[0]
    busy = place_ref[1]

    @pl.when(busy == 1)
    def _():
        gates = gate_ref[:, pl.ds(pl.multiple_of(head * HEAD_DIM, HEAD_DIM), HEAD_DIM)]
        level = lax.broadcasted_iota(jnp.int32, (LEVELS, HEAD_DIM), 0)
        place = lax.broadcasted_iota(jnp.int32, (rows, HEAD_DIM), 0)
        lane = lax.broadcasted_iota(jnp.int32, (rows, HEAD_DIM), 1)
        one = jnp.where(lane == 0, 1.0, 0.0).astype(jnp.bfloat16)
        ones = jnp.ones((rows, HEAD_DIM), jnp.bfloat16)

        def part(group, kind):
            return got_ref[pl.ds(group * per_group, per_group), kind].reshape(rows, HEAD_DIM)

        def score(c, d):
            return lax.dot_general(
                jnp.concatenate([part(c, 0), one], axis=1),
                jnp.concatenate([part(d, 1), bias_ref[d]], axis=1),
                (((1,), (1,)), ((), ())),
                preferred_element_type=jnp.float32,
            )

        def lane_top(scores, top):
            pieces = [scores[:, i : i + HEAD_DIM] for i in range(0, rows, HEAD_DIM)]
            return functools.reduce(jnp.maximum, pieces, top)

        def product(scores, top, d):
            shift = jnp.concatenate([top] * (rows // HEAD_DIM), axis=1)
            weights = jnp.exp(scores * factor - shift).astype(jnp.bfloat16)
            return jnp.dot(
                weights, jnp.concatenate([part(d, 2), ones], axis=1), preferred_element_type=jnp.float32
            )

        @pl.loop(0, GROUPS)
        def _(c):
            bias_ref[c] = jnp.where(place < counts_ref[c], 0.0, -1e30).astype(jnp.bfloat16)
            top_ref[...] = jnp.full(top_ref.shape, -1e30, jnp.float32)

            @pl.loop(0, c)
            def _(d):
                @pl.when(mask_ref[c, d] == 1)
                def _():
                    scores = score(c, d)
                    score_ref[d] = scores
                    top_ref[...] = lane_top(scores, top_ref[...])

            own = score(c, c)
            top = jnp.max(lane_top(own, top_ref[...]), axis=1, keepdims=True) * factor
            top = jnp.broadcast_to(top, top_ref.shape)
            top_ref[...] = top
            mixed_ref[...] = product(own, top, c)

            @pl.loop(0, c)
            def _(d):
                @pl.when(mask_ref[c, d] == 1)
                def _():
                    mixed_ref[...] += product(score_ref[d], top_ref[...], d)

            gate = jnp.sum(jnp.where(level == plan_ref[c], gates, jnp.float32(0.0)), axis=0, keepdims=True)
            mixed = mixed_ref[:, :HEAD_DIM] / mixed_ref[:, HEAD_DIM:] * gate
            mixed = jnp.where(place < counts_ref[c], mixed, jnp.float32(0.0))
            out_ref[pl.ds(c * per_group, per_group)] = mixed.astype(jnp.bfloat16).reshape(
                per_group, local, HEAD_DIM
            )

    @pl.when(busy == 0)
    def _():
        out_ref[...] = jnp.zeros_like(out_ref)


def head_each(queries, keys, values, counts, plan, group_mask, gate_table):
    axes = ("seq", "head")
    n_dev = lax.axis_size("seq") * lax.axis_size("head")
    local, feat = queries.shape
    heads = feat // HEAD_DIM
    parts = math.gcd(heads, n_dev)
    held, slots = heads // parts, n_dev // parts
    index = lax.axis_index("seq") * lax.axis_size("head") + lax.axis_index("head")
    lane = index % slots
    busy = (lane < held).astype(jnp.int32)
    head = jnp.minimum(index // slots * held + lane, heads - 1)
    place = jnp.stack([head, busy]).astype(jnp.int32)
    smem = pl.BlockSpec(memory_space=pltpu.SMEM)
    vmem = pl.BlockSpec(memory_space=pltpu.VMEM)

    sent = pack((queries, keys, values), parts, held, n_dev)
    got = lax.all_to_all(sent, axes, split_axis=0, concat_axis=0, tiled=True)
    rows = n_dev * local // GROUPS
    result = pl.pallas_call(
        attention_kernel,
        out_shape=jax.ShapeDtypeStruct((n_dev, local, HEAD_DIM), jnp.bfloat16),
        in_specs=[smem, smem, smem, smem, vmem, vmem],
        out_specs=vmem,
        scratch_shapes=[
            pltpu.VMEM((GROUPS, rows, HEAD_DIM), jnp.bfloat16),
            pltpu.VMEM((GROUPS - 1, rows, rows), jnp.float32),
            pltpu.VMEM((rows, HEAD_DIM), jnp.float32),
            pltpu.VMEM((rows, 2 * HEAD_DIM), jnp.float32),
        ],
        compiler_params=pltpu.CompilerParams(vmem_limit_bytes=40 * 1024 * 1024),
        name="attention",
    )(counts, plan, group_mask, place, got, gate_table)
    back = lax.all_to_all(result, axes, split_axis=0, concat_axis=0, tiled=True)
    return pl.pallas_call(
        functools.partial(unpack_kernel, parts, held),
        out_shape=jax.ShapeDtypeStruct((local, feat), jnp.bfloat16),
        in_specs=[vmem],
        out_specs=pl.BlockSpec(memory_space=pl.ANY),
        scratch_shapes=[pltpu.SemaphoreType.DMA],
        compiler_params=pltpu.CompilerParams(vmem_limit_bytes=16 * 1024 * 1024),
        name="unpack",
    )(back)


def on_device(queries, keys, values, counts, plan, group_mask, gate_table):
    n_dev = lax.axis_size("seq") * lax.axis_size("head")
    heads = queries.shape[1] // HEAD_DIM
    plan_of = head_each if heads <= n_dev <= 2 * heads else gathered
    return plan_of(queries, keys, values, counts, plan, group_mask, gate_table)


def solution(mesh):
    in_specs = (
        P(("seq", "head"), None),
        P(("seq", "head"), None),
        P(("seq", "head"), None),
        P(),
        P(),
        P(),
        P(),
    )
    out_specs = P(("seq", "head"), None)
    return jax.shard_map(
        on_device, mesh=mesh, in_specs=in_specs, out_specs=out_specs, check_vma=False
    )
```

```python
import functools
import math

import jax
import jax.numpy as jnp
from jax import lax
from jax.experimental import pallas as pl
from jax.experimental.pallas import tpu as pltpu
from jax.sharding import PartitionSpec as P

HEAD_DIM = 128
GROUPS = 4
LEVELS = 8


def lookup(table, index):
    hits = index[:, None] == jnp.arange(table.shape[0], dtype=jnp.int32)[None, :]
    return jnp.sum(jnp.where(hits, table[None, :], 0), axis=1)


def attend(
    work_q, k_local, v_local, row_group, row_pos, counts, plan, group_mask, gate_slice, group_tok
):
    rows = work_q.shape[0]
    width = work_q.shape[1]
    heads_here = width // HEAD_DIM
    scale = 1.0 / math.sqrt(HEAD_DIM)
    q_three = work_q.reshape(rows, heads_here, HEAD_DIM)
    row_onehot = (row_group[:, None] == jnp.arange(GROUPS, dtype=jnp.int32)[None, :]).astype(
        jnp.float32
    )
    mask_rows = jnp.dot(row_onehot, group_mask.astype(jnp.float32))
    k_piece = lax.all_gather(k_local, "seq", axis=0, tiled=True)
    v_piece = lax.all_gather(v_local, "seq", axis=0, tiled=True)
    count = k_piece.shape[0]
    index = jnp.arange(count, dtype=jnp.int32)
    k_group = index // group_tok
    k_pos = index % group_tok
    k_onehot = (k_group[:, None] == jnp.arange(GROUPS, dtype=jnp.int32)[None, :]).astype(
        jnp.float32
    )
    k_valid = k_pos < lookup(counts, k_group)
    allowed = (jnp.dot(mask_rows, k_onehot.T) > 0.5) & k_valid[None, :]
    running = jnp.full((heads_here, rows), -1e30, jnp.float32)
    k_three = k_piece.reshape(count, heads_here, HEAD_DIM)
    v_three = v_piece.reshape(count, heads_here, HEAD_DIM)
    scores = (
        jnp.einsum("qhd,khd->hqk", q_three, k_three, preferred_element_type=jnp.float32) * scale
    )
    scores = jnp.where(allowed[None], scores, jnp.float32(-1e30))
    newest = jnp.maximum(running, jnp.max(scores, axis=2))
    weights = jnp.exp(scores - newest[:, :, None]) * allowed[None].astype(jnp.float32)
    total = jnp.sum(weights, axis=2)
    rounded = weights.astype(jnp.bfloat16)
    accum = jnp.einsum("hqk,khd->hqd", rounded, v_three, preferred_element_type=jnp.float32)
    running, total, accum = (newest, total, accum)
    mixed = accum / total[:, :, None]
    mixed = jnp.transpose(mixed, (1, 0, 2)).reshape(rows, width)
    level_rows = lookup(plan, row_group)
    level_hits = level_rows[:, None] == jnp.arange(LEVELS, dtype=jnp.int32)[None, :]
    gates = jnp.sum(
        jnp.where(level_hits[:, :, None], gate_slice[None, :, :], jnp.float32(0.0)), axis=1
    )
    live = row_pos < lookup(counts, row_group)
    return jnp.where(live[:, None], mixed * gates, jnp.float32(0.0)).astype(jnp.bfloat16)


def gathered(queries, keys, values, counts, plan, group_mask, gate_table):
    n_seq = lax.axis_size("seq")
    n_head = lax.axis_size("head")
    per_group = n_seq // GROUPS
    tok_dev = queries.shape[0] * n_head
    group_tok = tok_dev * per_group
    q_local, k_local, v_local = (
        lax.all_to_all(queries, "head", split_axis=1, concat_axis=0, tiled=True),
        lax.all_to_all(keys, "head", split_axis=1, concat_axis=0, tiled=True),
        lax.all_to_all(values, "head", split_axis=1, concat_axis=0, tiled=True),
    )
    width = q_local.shape[1]
    seq_index = lax.axis_index("seq")
    own_group = seq_index // per_group
    positions = seq_index % per_group * tok_dev + jnp.arange(tok_dev, dtype=jnp.int32)
    gate_slice = lax.dynamic_slice_in_dim(gate_table, lax.axis_index("head") * width, width, 1)
    row_group = jnp.full((tok_dev,), own_group, jnp.int32)
    result = attend(
        q_local,
        k_local,
        v_local,
        row_group,
        positions,
        counts,
        plan,
        group_mask,
        gate_slice,
        group_tok,
    )
    return lax.all_to_all(result, "head", split_axis=0, concat_axis=1, tiled=True)


def pack_kernel(parts, held, q_ref, k_ref, v_ref, out_ref, in_buf, out_buf, in_sem, out_sem):
    slots = out_ref.shape[0] // parts
    arrays = (q_ref, k_ref, v_ref)
    copies = [pltpu.make_async_copy(ref, in_buf.at[i], in_sem.at[i]) for i, ref in enumerate(arrays)]
    for copy in copies:
        copy.start()
    for s in range(held, slots):
        for p in range(parts):
            for i in range(len(arrays)):
                out_buf[i, p * slots + s] = jnp.zeros(out_buf.shape[2:], out_buf.dtype)
    stores = []
    for i, copy in enumerate(copies):
        copy.wait()
        for p in range(parts):
            for s in range(held):
                h = p * held + s
                out_buf[i, p * slots + s] = in_buf[i, :, h * HEAD_DIM : (h + 1) * HEAD_DIM]
        stores.append(pltpu.make_async_copy(out_buf.at[i], out_ref.at[:, i], out_sem.at[i]))
        stores[-1].start()
    for store in stores:
        store.wait()


def pack(arrays, parts, held, n_dev):
    local, feat = arrays[0].shape
    count = len(arrays)
    return pl.pallas_call(
        functools.partial(pack_kernel, parts, held),
        out_shape=jax.ShapeDtypeStruct((n_dev, count, local, HEAD_DIM), jnp.bfloat16),
        in_specs=[pl.BlockSpec(memory_space=pl.ANY)] * count,
        out_specs=pl.BlockSpec(memory_space=pl.ANY),
        scratch_shapes=[
            pltpu.VMEM((count, local, feat), jnp.bfloat16),
            pltpu.VMEM((count, n_dev, local, HEAD_DIM), jnp.bfloat16),
            pltpu.SemaphoreType.DMA((count,)),
            pltpu.SemaphoreType.DMA((count,)),
        ],
        compiler_params=pltpu.CompilerParams(vmem_limit_bytes=60 * 1024 * 1024),
        name="pack",
    )(*arrays)


def unpack_kernel(parts, held, in_ref, out_ref, sem):
    slots = in_ref.shape[0] // parts
    for p in range(parts):
        for s in range(held):
            h = p * held + s
            pltpu.make_async_copy(
                in_ref.at[p * slots + s], out_ref.at[:, h * HEAD_DIM : (h + 1) * HEAD_DIM], sem
            ).start()
    pltpu.make_async_copy(out_ref, out_ref, sem).wait()


def attention_kernel(
    info_ref, got_ref, gate_ref, out_ref, bias_ref, score_ref, top_ref, mixed_ref
):
    n_dev, _, local, _ = got_ref.shape
    per_group = n_dev // GROUPS
    rows = per_group * local
    factor = 1.0 / math.sqrt(HEAD_DIM)
    head = info_ref[0]
    busy = info_ref[1]

    def count_of(group):
        return info_ref[2 + group]

    def level_of(group):
        return info_ref[2 + GROUPS + group]

    def sees(group, other):
        return info_ref[2 + 2 * GROUPS + group * GROUPS + other] == 1

    @pl.when(busy == 1)
    def _():
        gates = gate_ref[:, pl.ds(pl.multiple_of(head * HEAD_DIM, HEAD_DIM), HEAD_DIM)]
        level = lax.broadcasted_iota(jnp.int32, (LEVELS, HEAD_DIM), 0)
        place = lax.broadcasted_iota(jnp.int32, (rows, HEAD_DIM), 0)
        lane = lax.broadcasted_iota(jnp.int32, (rows, HEAD_DIM), 1)
        one = jnp.where(lane == 0, 1.0, 0.0).astype(jnp.bfloat16)
        ones = jnp.ones((rows, HEAD_DIM), jnp.bfloat16)

        def part(group, kind):
            return got_ref[pl.ds(group * per_group, per_group), kind].reshape(rows, HEAD_DIM)

        def score(c, d):
            return lax.dot_general(
                jnp.concatenate([part(c, 0), one], axis=1),
                jnp.concatenate([part(d, 1), bias_ref[d]], axis=1),
                (((1,), (1,)), ((), ())),
                preferred_element_type=jnp.float32,
            )

        def lane_top(scores, top):
            pieces = [scores[:, i : i + HEAD_DIM] for i in range(0, rows, HEAD_DIM)]
            return functools.reduce(jnp.maximum, pieces, top)

        def product(scores, top, d):
            shift = jnp.concatenate([top] * (rows // HEAD_DIM), axis=1)
            weights = jnp.exp(scores * factor - shift).astype(jnp.bfloat16)
            return jnp.dot(
                weights, jnp.concatenate([part(d, 2), ones], axis=1), preferred_element_type=jnp.float32
            )

        @pl.loop(0, GROUPS)
        def _(c):
            bias_ref[c] = jnp.where(place < count_of(c), 0.0, -1e30).astype(jnp.bfloat16)
            top_ref[...] = jnp.full(top_ref.shape, -1e30, jnp.float32)

            @pl.loop(0, c)
            def _(d):
                @pl.when(sees(c, d))
                def _():
                    scores = score(c, d)
                    score_ref[d] = scores
                    top_ref[...] = lane_top(scores, top_ref[...])

            own = score(c, c)
            top = jnp.max(lane_top(own, top_ref[...]), axis=1, keepdims=True) * factor
            top = jnp.broadcast_to(top, top_ref.shape)
            top_ref[...] = top
            mixed_ref[...] = product(own, top, c)

            @pl.loop(0, c)
            def _(d):
                @pl.when(sees(c, d))
                def _():
                    mixed_ref[...] += product(score_ref[d], top_ref[...], d)

            gate = jnp.sum(jnp.where(level == level_of(c), gates, jnp.float32(0.0)), axis=0, keepdims=True)
            mixed = mixed_ref[:, :HEAD_DIM] / mixed_ref[:, HEAD_DIM:] * gate
            mixed = jnp.where(place < count_of(c), mixed, jnp.float32(0.0))
            out_ref[pl.ds(c * per_group, per_group)] = mixed.astype(jnp.bfloat16).reshape(
                per_group, local, HEAD_DIM
            )

    @pl.when(busy == 0)
    def _():
        out_ref[...] = jnp.zeros_like(out_ref)


def head_each(queries, keys, values, counts, plan, group_mask, gate_table):
    axes = ("seq", "head")
    n_dev = lax.axis_size("seq") * lax.axis_size("head")
    local, feat = queries.shape
    heads = feat // HEAD_DIM
    parts = math.gcd(heads, n_dev)
    held, slots = heads // parts, n_dev // parts
    index = lax.axis_index("seq") * lax.axis_size("head") + lax.axis_index("head")
    lane = index % slots
    busy = (lane < held).astype(jnp.int32)
    head = jnp.minimum(index // slots * held + lane, heads - 1)
    place = jnp.stack([head, busy]).astype(jnp.int32)
    info = jnp.concatenate([place, counts, plan, group_mask.reshape(-1)])
    smem = pl.BlockSpec(memory_space=pltpu.SMEM)
    vmem = pl.BlockSpec(memory_space=pltpu.VMEM)

    sent = pack((queries, keys, values), parts, held, n_dev)
    got = lax.all_to_all(sent, axes, split_axis=0, concat_axis=0, tiled=True)
    rows = n_dev * local // GROUPS
    result = pl.pallas_call(
        attention_kernel,
        out_shape=jax.ShapeDtypeStruct((n_dev, local, HEAD_DIM), jnp.bfloat16),
        in_specs=[smem, vmem, vmem],
        out_specs=vmem,
        scratch_shapes=[
            pltpu.VMEM((GROUPS, rows, HEAD_DIM), jnp.bfloat16),
            pltpu.VMEM((GROUPS - 1, rows, rows), jnp.float32),
            pltpu.VMEM((rows, HEAD_DIM), jnp.float32),
            pltpu.VMEM((rows, 2 * HEAD_DIM), jnp.float32),
        ],
        compiler_params=pltpu.CompilerParams(vmem_limit_bytes=40 * 1024 * 1024),
        name="attention",
    )(info, got, gate_table)
    back = lax.all_to_all(result, axes, split_axis=0, concat_axis=0, tiled=True)
    return pl.pallas_call(
        functools.partial(unpack_kernel, parts, held),
        out_shape=jax.ShapeDtypeStruct((local, feat), jnp.bfloat16),
        in_specs=[vmem],
        out_specs=pl.BlockSpec(memory_space=pl.ANY),
        scratch_shapes=[pltpu.SemaphoreType.DMA],
        compiler_params=pltpu.CompilerParams(vmem_limit_bytes=16 * 1024 * 1024),
        name="unpack",
    )(back)


def on_device(queries, keys, values, counts, plan, group_mask, gate_table):
    n_dev = lax.axis_size("seq") * lax.axis_size("head")
    heads = queries.shape[1] // HEAD_DIM
    plan_of = head_each if heads <= n_dev <= 2 * heads else gathered
    return plan_of(queries, keys, values, counts, plan, group_mask, gate_table)


def solution(mesh):
    in_specs = (
        P(("seq", "head"), None),
        P(("seq", "head"), None),
        P(("seq", "head"), None),
        P(),
        P(),
        P(),
        P(),
    )
    out_specs = P(("seq", "head"), None)
    return jax.shard_map(
        on_device, mesh=mesh, in_specs=in_specs, out_specs=out_specs, check_vma=False
    )
```

```python
import functools
import math

import jax
import jax.numpy as jnp
from jax import lax
from jax.experimental import pallas as pl
from jax.experimental.pallas import tpu as pltpu
from jax.sharding import PartitionSpec as P

HEAD_DIM = 128
GROUPS = 4
LEVELS = 8


def lookup(table, index):
    hits = index[:, None] == jnp.arange(table.shape[0], dtype=jnp.int32)[None, :]
    return jnp.sum(jnp.where(hits, table[None, :], 0), axis=1)


def attend(
    work_q, k_local, v_local, row_group, row_pos, counts, plan, group_mask, gate_slice, group_tok
):
    rows = work_q.shape[0]
    width = work_q.shape[1]
    heads_here = width // HEAD_DIM
    scale = 1.0 / math.sqrt(HEAD_DIM)
    q_three = work_q.reshape(rows, heads_here, HEAD_DIM)
    row_onehot = (row_group[:, None] == jnp.arange(GROUPS, dtype=jnp.int32)[None, :]).astype(
        jnp.float32
    )
    mask_rows = jnp.dot(row_onehot, group_mask.astype(jnp.float32))
    k_piece = lax.all_gather(k_local, "seq", axis=0, tiled=True)
    v_piece = lax.all_gather(v_local, "seq", axis=0, tiled=True)
    count = k_piece.shape[0]
    index = jnp.arange(count, dtype=jnp.int32)
    k_group = index // group_tok
    k_pos = index % group_tok
    k_onehot = (k_group[:, None] == jnp.arange(GROUPS, dtype=jnp.int32)[None, :]).astype(
        jnp.float32
    )
    k_valid = k_pos < lookup(counts, k_group)
    allowed = (jnp.dot(mask_rows, k_onehot.T) > 0.5) & k_valid[None, :]
    running = jnp.full((heads_here, rows), -1e30, jnp.float32)
    k_three = k_piece.reshape(count, heads_here, HEAD_DIM)
    v_three = v_piece.reshape(count, heads_here, HEAD_DIM)
    scores = (
        jnp.einsum("qhd,khd->hqk", q_three, k_three, preferred_element_type=jnp.float32) * scale
    )
    scores = jnp.where(allowed[None], scores, jnp.float32(-1e30))
    newest = jnp.maximum(running, jnp.max(scores, axis=2))
    weights = jnp.exp(scores - newest[:, :, None]) * allowed[None].astype(jnp.float32)
    total = jnp.sum(weights, axis=2)
    rounded = weights.astype(jnp.bfloat16)
    accum = jnp.einsum("hqk,khd->hqd", rounded, v_three, preferred_element_type=jnp.float32)
    running, total, accum = (newest, total, accum)
    mixed = accum / total[:, :, None]
    mixed = jnp.transpose(mixed, (1, 0, 2)).reshape(rows, width)
    level_rows = lookup(plan, row_group)
    level_hits = level_rows[:, None] == jnp.arange(LEVELS, dtype=jnp.int32)[None, :]
    gates = jnp.sum(
        jnp.where(level_hits[:, :, None], gate_slice[None, :, :], jnp.float32(0.0)), axis=1
    )
    live = row_pos < lookup(counts, row_group)
    return jnp.where(live[:, None], mixed * gates, jnp.float32(0.0)).astype(jnp.bfloat16)


def gathered(queries, keys, values, counts, plan, group_mask, gate_table):
    n_seq = lax.axis_size("seq")
    n_head = lax.axis_size("head")
    per_group = n_seq // GROUPS
    tok_dev = queries.shape[0] * n_head
    group_tok = tok_dev * per_group
    q_local, k_local, v_local = (
        lax.all_to_all(queries, "head", split_axis=1, concat_axis=0, tiled=True),
        lax.all_to_all(keys, "head", split_axis=1, concat_axis=0, tiled=True),
        lax.all_to_all(values, "head", split_axis=1, concat_axis=0, tiled=True),
    )
    width = q_local.shape[1]
    seq_index = lax.axis_index("seq")
    own_group = seq_index // per_group
    positions = seq_index % per_group * tok_dev + jnp.arange(tok_dev, dtype=jnp.int32)
    gate_slice = lax.dynamic_slice_in_dim(gate_table, lax.axis_index("head") * width, width, 1)
    row_group = jnp.full((tok_dev,), own_group, jnp.int32)
    result = attend(
        q_local,
        k_local,
        v_local,
        row_group,
        positions,
        counts,
        plan,
        group_mask,
        gate_slice,
        group_tok,
    )
    return lax.all_to_all(result, "head", split_axis=0, concat_axis=1, tiled=True)


def pack_kernel(parts, held, q_ref, k_ref, v_ref, out_ref, in_buf, out_buf, in_sem, out_sem):
    slots = out_ref.shape[0] // parts
    arrays = (q_ref, k_ref, v_ref)
    copies = [pltpu.make_async_copy(ref, in_buf.at[i], in_sem.at[i]) for i, ref in enumerate(arrays)]
    for copy in copies:
        copy.start()
    for s in range(held, slots):
        for p in range(parts):
            for i in range(len(arrays)):
                out_buf[i, p * slots + s] = jnp.zeros(out_buf.shape[2:], out_buf.dtype)
    stores = []
    for i, copy in enumerate(copies):
        copy.wait()
        for p in range(parts):
            for s in range(held):
                h = p * held + s
                out_buf[i, p * slots + s] = in_buf[i, :, h * HEAD_DIM : (h + 1) * HEAD_DIM]
        stores.append(pltpu.make_async_copy(out_buf.at[i], out_ref.at[:, i], out_sem.at[i]))
        stores[-1].start()
    for store in stores:
        store.wait()


def pack(arrays, parts, held, n_dev):
    local, feat = arrays[0].shape
    count = len(arrays)
    return pl.pallas_call(
        functools.partial(pack_kernel, parts, held),
        out_shape=jax.ShapeDtypeStruct((n_dev, count, local, HEAD_DIM), jnp.bfloat16),
        in_specs=[pl.BlockSpec(memory_space=pl.ANY)] * count,
        out_specs=pl.BlockSpec(memory_space=pl.ANY),
        scratch_shapes=[
            pltpu.VMEM((count, local, feat), jnp.bfloat16),
            pltpu.VMEM((count, n_dev, local, HEAD_DIM), jnp.bfloat16),
            pltpu.SemaphoreType.DMA((count,)),
            pltpu.SemaphoreType.DMA((count,)),
        ],
        compiler_params=pltpu.CompilerParams(vmem_limit_bytes=60 * 1024 * 1024),
        name="pack",
    )(*arrays)


def unpack_kernel(parts, held, in_ref, out_ref, sem):
    slots = in_ref.shape[0] // parts
    for p in range(parts):
        for s in range(held):
            h = p * held + s
            pltpu.make_async_copy(
                in_ref.at[p * slots + s], out_ref.at[:, h * HEAD_DIM : (h + 1) * HEAD_DIM], sem
            ).start()
    pltpu.make_async_copy(out_ref, out_ref, sem).wait()


def attention_kernel(
    info_ref, got_ref, gate_ref, out_ref, bias_ref, score_ref, mixed_ref, *pair_refs
):
    n_dev, _, local, _ = got_ref.shape
    per_group = n_dev // GROUPS
    rows = per_group * local
    factor = 1.0 / math.sqrt(HEAD_DIM)
    own_refs, top_refs = pair_refs[:2], pair_refs[2:]
    head = info_ref[0]
    busy = info_ref[1]

    def count_of(group):
        return info_ref[2 + group]

    def level_of(group):
        return info_ref[2 + GROUPS + group]

    def sees(group, other):
        return info_ref[2 + 2 * GROUPS + group * GROUPS + other] == 1

    @pl.when(busy == 1)
    def _():
        gates = gate_ref[:, pl.ds(pl.multiple_of(head * HEAD_DIM, HEAD_DIM), HEAD_DIM)]
        level = lax.broadcasted_iota(jnp.int32, (LEVELS, HEAD_DIM), 0)
        place = lax.broadcasted_iota(jnp.int32, (rows, HEAD_DIM), 0)
        lane = lax.broadcasted_iota(jnp.int32, (rows, HEAD_DIM), 1)
        one = jnp.where(lane == 0, 1.0, 0.0).astype(jnp.bfloat16)
        ones = jnp.ones((rows, HEAD_DIM), jnp.bfloat16)

        def part(group, kind):
            return got_ref[pl.ds(group * per_group, per_group), kind].reshape(rows, HEAD_DIM)

        def score(c, d):
            return lax.dot_general(
                jnp.concatenate([part(c, 0), one], axis=1),
                jnp.concatenate([part(d, 1), bias_ref[d]], axis=1),
                (((1,), (1,)), ((), ())),
                preferred_element_type=jnp.float32,
            )

        def lane_top(scores, top):
            pieces = [scores[:, i : i + HEAD_DIM] for i in range(0, rows, HEAD_DIM)]
            return functools.reduce(jnp.maximum, pieces, top)

        def product(scores, top, d):
            shift = jnp.concatenate([top] * (rows // HEAD_DIM), axis=1)
            weights = jnp.exp(scores * factor - shift).astype(jnp.bfloat16)
            return jnp.dot(
                weights, jnp.concatenate([part(d, 2), ones], axis=1), preferred_element_type=jnp.float32
            )

        def own_scores(c):
            scores = score(c, c)
            own_refs[c % 2][...] = scores
            top_refs[c % 2][...] = lane_top(scores, jnp.float32(-1e30))

        for c in range(GROUPS):
            bias_ref[c] = jnp.where(place < count_of(c), 0.0, -1e30).astype(jnp.bfloat16)
        own_scores(0)
        for c in range(GROUPS):
            top_ref = top_refs[c % 2]

            @pl.loop(0, c)
            def _(d):
                @pl.when(sees(c, d))
                def _():
                    scores = score(c, d)
                    score_ref[d] = scores
                    top_ref[...] = lane_top(scores, top_ref[...])

            top = jnp.max(top_ref[...], axis=1, keepdims=True) * factor
            top = jnp.broadcast_to(top, top_ref.shape)
            top_ref[...] = top
            if c + 1 < GROUPS:
                own_scores(c + 1)
            mixed_ref[...] = product(own_refs[c % 2][...], top, c)

            @pl.loop(0, c)
            def _(d):
                @pl.when(sees(c, d))
                def _():
                    mixed_ref[...] += product(score_ref[d], top_ref[...], d)

            gate = jnp.sum(jnp.where(level == level_of(c), gates, jnp.float32(0.0)), axis=0, keepdims=True)
            mixed = mixed_ref[:, :HEAD_DIM] / mixed_ref[:, HEAD_DIM:] * gate
            mixed = jnp.where(place < count_of(c), mixed, jnp.float32(0.0))
            out_ref[c * per_group : (c + 1) * per_group] = mixed.astype(jnp.bfloat16).reshape(
                per_group, local, HEAD_DIM
            )

    @pl.when(busy == 0)
    def _():
        out_ref[...] = jnp.zeros_like(out_ref)


def head_each(queries, keys, values, counts, plan, group_mask, gate_table):
    axes = ("seq", "head")
    n_dev = lax.axis_size("seq") * lax.axis_size("head")
    local, feat = queries.shape
    heads = feat // HEAD_DIM
    parts = math.gcd(heads, n_dev)
    held, slots = heads // parts, n_dev // parts
    index = lax.axis_index("seq") * lax.axis_size("head") + lax.axis_index("head")
    lane = index % slots
    busy = (lane < held).astype(jnp.int32)
    head = jnp.minimum(index // slots * held + lane, heads - 1)
    place = jnp.stack([head, busy]).astype(jnp.int32)
    info = jnp.concatenate([place, counts, plan, group_mask.reshape(-1)])
    smem = pl.BlockSpec(memory_space=pltpu.SMEM)
    vmem = pl.BlockSpec(memory_space=pltpu.VMEM)

    sent = pack((queries, keys, values), parts, held, n_dev)
    got = lax.all_to_all(sent, axes, split_axis=0, concat_axis=0, tiled=True)
    rows = n_dev * local // GROUPS
    result = pl.pallas_call(
        attention_kernel,
        out_shape=jax.ShapeDtypeStruct((n_dev, local, HEAD_DIM), jnp.bfloat16),
        in_specs=[smem, vmem, vmem],
        out_specs=vmem,
        scratch_shapes=[
            pltpu.VMEM((GROUPS, rows, HEAD_DIM), jnp.bfloat16),
            pltpu.VMEM((GROUPS - 1, rows, rows), jnp.float32),
            pltpu.VMEM((rows, 2 * HEAD_DIM), jnp.float32),
            pltpu.VMEM((rows, rows), jnp.float32),
            pltpu.VMEM((rows, rows), jnp.float32),
            pltpu.VMEM((rows, HEAD_DIM), jnp.float32),
            pltpu.VMEM((rows, HEAD_DIM), jnp.float32),
        ],
        compiler_params=pltpu.CompilerParams(vmem_limit_bytes=40 * 1024 * 1024),
        name="attention",
    )(info, got, gate_table)
    back = lax.all_to_all(result, axes, split_axis=0, concat_axis=0, tiled=True)
    return pl.pallas_call(
        functools.partial(unpack_kernel, parts, held),
        out_shape=jax.ShapeDtypeStruct((local, feat), jnp.bfloat16),
        in_specs=[vmem],
        out_specs=pl.BlockSpec(memory_space=pl.ANY),
        scratch_shapes=[pltpu.SemaphoreType.DMA],
        compiler_params=pltpu.CompilerParams(vmem_limit_bytes=16 * 1024 * 1024),
        name="unpack",
    )(back)


def on_device(queries, keys, values, counts, plan, group_mask, gate_table):
    n_dev = lax.axis_size("seq") * lax.axis_size("head")
    heads = queries.shape[1] // HEAD_DIM
    plan_of = head_each if heads <= n_dev <= 2 * heads else gathered
    return plan_of(queries, keys, values, counts, plan, group_mask, gate_table)


def solution(mesh):
    in_specs = (
        P(("seq", "head"), None),
        P(("seq", "head"), None),
        P(("seq", "head"), None),
        P(),
        P(),
        P(),
        P(),
    )
    out_specs = P(("seq", "head"), None)
    return jax.shard_map(
        on_device, mesh=mesh, in_specs=in_specs, out_specs=out_specs, check_vma=False
    )
```

```python
import functools
import math

import jax
import jax.numpy as jnp
from jax import lax
from jax.experimental import pallas as pl
from jax.experimental.pallas import tpu as pltpu
from jax.sharding import PartitionSpec as P

HEAD_DIM = 128
GROUPS = 4
LEVELS = 8


def lookup(table, index):
    hits = index[:, None] == jnp.arange(table.shape[0], dtype=jnp.int32)[None, :]
    return jnp.sum(jnp.where(hits, table[None, :], 0), axis=1)


def attend(
    work_q, k_local, v_local, row_group, row_pos, counts, plan, group_mask, gate_slice, group_tok
):
    rows = work_q.shape[0]
    width = work_q.shape[1]
    heads_here = width // HEAD_DIM
    scale = 1.0 / math.sqrt(HEAD_DIM)
    q_three = work_q.reshape(rows, heads_here, HEAD_DIM)
    row_onehot = (row_group[:, None] == jnp.arange(GROUPS, dtype=jnp.int32)[None, :]).astype(
        jnp.float32
    )
    mask_rows = jnp.dot(row_onehot, group_mask.astype(jnp.float32))
    k_piece = lax.all_gather(k_local, "seq", axis=0, tiled=True)
    v_piece = lax.all_gather(v_local, "seq", axis=0, tiled=True)
    count = k_piece.shape[0]
    index = jnp.arange(count, dtype=jnp.int32)
    k_group = index // group_tok
    k_pos = index % group_tok
    k_onehot = (k_group[:, None] == jnp.arange(GROUPS, dtype=jnp.int32)[None, :]).astype(
        jnp.float32
    )
    k_valid = k_pos < lookup(counts, k_group)
    allowed = (jnp.dot(mask_rows, k_onehot.T) > 0.5) & k_valid[None, :]
    running = jnp.full((heads_here, rows), -1e30, jnp.float32)
    k_three = k_piece.reshape(count, heads_here, HEAD_DIM)
    v_three = v_piece.reshape(count, heads_here, HEAD_DIM)
    scores = (
        jnp.einsum("qhd,khd->hqk", q_three, k_three, preferred_element_type=jnp.float32) * scale
    )
    scores = jnp.where(allowed[None], scores, jnp.float32(-1e30))
    newest = jnp.maximum(running, jnp.max(scores, axis=2))
    weights = jnp.exp(scores - newest[:, :, None]) * allowed[None].astype(jnp.float32)
    total = jnp.sum(weights, axis=2)
    rounded = weights.astype(jnp.bfloat16)
    accum = jnp.einsum("hqk,khd->hqd", rounded, v_three, preferred_element_type=jnp.float32)
    running, total, accum = (newest, total, accum)
    mixed = accum / total[:, :, None]
    mixed = jnp.transpose(mixed, (1, 0, 2)).reshape(rows, width)
    level_rows = lookup(plan, row_group)
    level_hits = level_rows[:, None] == jnp.arange(LEVELS, dtype=jnp.int32)[None, :]
    gates = jnp.sum(
        jnp.where(level_hits[:, :, None], gate_slice[None, :, :], jnp.float32(0.0)), axis=1
    )
    live = row_pos < lookup(counts, row_group)
    return jnp.where(live[:, None], mixed * gates, jnp.float32(0.0)).astype(jnp.bfloat16)


def gathered(queries, keys, values, counts, plan, group_mask, gate_table):
    n_seq = lax.axis_size("seq")
    n_head = lax.axis_size("head")
    per_group = n_seq // GROUPS
    tok_dev = queries.shape[0] * n_head
    group_tok = tok_dev * per_group
    q_local, k_local, v_local = (
        lax.all_to_all(queries, "head", split_axis=1, concat_axis=0, tiled=True),
        lax.all_to_all(keys, "head", split_axis=1, concat_axis=0, tiled=True),
        lax.all_to_all(values, "head", split_axis=1, concat_axis=0, tiled=True),
    )
    width = q_local.shape[1]
    seq_index = lax.axis_index("seq")
    own_group = seq_index // per_group
    positions = seq_index % per_group * tok_dev + jnp.arange(tok_dev, dtype=jnp.int32)
    gate_slice = lax.dynamic_slice_in_dim(gate_table, lax.axis_index("head") * width, width, 1)
    row_group = jnp.full((tok_dev,), own_group, jnp.int32)
    result = attend(
        q_local,
        k_local,
        v_local,
        row_group,
        positions,
        counts,
        plan,
        group_mask,
        gate_slice,
        group_tok,
    )
    return lax.all_to_all(result, "head", split_axis=0, concat_axis=1, tiled=True)


def pack_kernel(parts, held, q_ref, k_ref, v_ref, out_ref, in_buf, out_buf, in_sem, out_sem):
    slots = out_ref.shape[0] // parts
    arrays = (q_ref, k_ref, v_ref)
    copies = [pltpu.make_async_copy(ref, in_buf.at[i], in_sem.at[i]) for i, ref in enumerate(arrays)]
    for copy in copies:
        copy.start()
    for s in range(held, slots):
        for p in range(parts):
            for i in range(len(arrays)):
                out_buf[i, p * slots + s] = jnp.zeros(out_buf.shape[2:], out_buf.dtype)
    stores = []
    for i, copy in enumerate(copies):
        copy.wait()
        for p in range(parts):
            for s in range(held):
                h = p * held + s
                out_buf[i, p * slots + s] = in_buf[i, :, h * HEAD_DIM : (h + 1) * HEAD_DIM]
        stores.append(pltpu.make_async_copy(out_buf.at[i], out_ref.at[:, i], out_sem.at[i]))
        stores[-1].start()
    for store in stores:
        store.wait()


def pack(arrays, parts, held, n_dev):
    local, feat = arrays[0].shape
    count = len(arrays)
    return pl.pallas_call(
        functools.partial(pack_kernel, parts, held),
        out_shape=jax.ShapeDtypeStruct((n_dev, count, local, HEAD_DIM), jnp.bfloat16),
        in_specs=[pl.BlockSpec(memory_space=pl.ANY)] * count,
        out_specs=pl.BlockSpec(memory_space=pl.ANY),
        scratch_shapes=[
            pltpu.VMEM((count, local, feat), jnp.bfloat16),
            pltpu.VMEM((count, n_dev, local, HEAD_DIM), jnp.bfloat16),
            pltpu.SemaphoreType.DMA((count,)),
            pltpu.SemaphoreType.DMA((count,)),
        ],
        compiler_params=pltpu.CompilerParams(vmem_limit_bytes=60 * 1024 * 1024),
        name="pack",
    )(*arrays)


def unpack_kernel(parts, held, in_ref, out_ref, sem):
    slots = in_ref.shape[0] // parts
    for p in range(parts):
        for s in range(held):
            h = p * held + s
            pltpu.make_async_copy(
                in_ref.at[p * slots + s], out_ref.at[:, h * HEAD_DIM : (h + 1) * HEAD_DIM], sem
            ).start()
    pltpu.make_async_copy(out_ref, out_ref, sem).wait()


def attention_kernel(
    info_ref, got_ref, gate_ref, out_ref, bias_ref, score_ref, mixed_ref, sum_ref, *pair_refs
):
    n_dev, _, local, _ = got_ref.shape
    per_group = n_dev // GROUPS
    rows = per_group * local
    factor = 1.0 / math.sqrt(HEAD_DIM)
    own_refs, top_refs = pair_refs[:2], pair_refs[2:]
    head = info_ref[0]
    busy = info_ref[1]

    def count_of(group):
        return info_ref[2 + group]

    def level_of(group):
        return info_ref[2 + GROUPS + group]

    def sees(group, other):
        return info_ref[2 + 2 * GROUPS + group * GROUPS + other] == 1

    @pl.when(busy == 1)
    def _():
        gates = gate_ref[:, pl.ds(pl.multiple_of(head * HEAD_DIM, HEAD_DIM), HEAD_DIM)]
        level = lax.broadcasted_iota(jnp.int32, (LEVELS, HEAD_DIM), 0)
        place = lax.broadcasted_iota(jnp.int32, (rows, HEAD_DIM), 0)
        lane = lax.broadcasted_iota(jnp.int32, (rows, HEAD_DIM), 1)
        one = jnp.where(lane == 0, 1.0, 0.0).astype(jnp.bfloat16)

        def part(group, kind):
            return got_ref[pl.ds(group * per_group, per_group), kind].reshape(rows, HEAD_DIM)

        def score(c, d):
            return lax.dot_general(
                jnp.concatenate([part(c, 0), one], axis=1),
                jnp.concatenate([part(d, 1), bias_ref[d]], axis=1),
                (((1,), (1,)), ((), ())),
                preferred_element_type=jnp.float32,
            )

        def lane_top(scores, top):
            pieces = [scores[:, i : i + HEAD_DIM] for i in range(0, rows, HEAD_DIM)]
            return functools.reduce(jnp.maximum, pieces, top)

        def product(scores, top, d):
            shift = jnp.concatenate([top] * (rows // HEAD_DIM), axis=1)
            weights = jnp.exp(scores * factor - shift)
            pieces = [weights[:, i : i + HEAD_DIM] for i in range(0, rows, HEAD_DIM)]
            return functools.reduce(jnp.add, pieces), jnp.dot(
                weights.astype(jnp.bfloat16), part(d, 2), preferred_element_type=jnp.float32
            )

        def own_scores(c):
            scores = score(c, c)
            own_refs[c % 2][...] = scores
            top_refs[c % 2][...] = lane_top(scores, jnp.float32(-1e30))

        for c in range(GROUPS):
            bias_ref[c] = jnp.where(place < count_of(c), 0.0, -1e30).astype(jnp.bfloat16)
        own_scores(0)
        for c in range(GROUPS):
            top_ref = top_refs[c % 2]

            @pl.loop(0, c)
            def _(d):
                @pl.when(sees(c, d))
                def _():
                    scores = score(c, d)
                    score_ref[d] = scores
                    top_ref[...] = lane_top(scores, top_ref[...])

            top = jnp.max(top_ref[...], axis=1, keepdims=True) * factor
            top = jnp.broadcast_to(top, top_ref.shape)
            top_ref[...] = top
            if c + 1 < GROUPS:
                own_scores(c + 1)
            sum_ref[...], mixed_ref[...] = product(own_refs[c % 2][...], top, c)

            @pl.loop(0, c)
            def _(d):
                @pl.when(sees(c, d))
                def _():
                    sums, mixed = product(score_ref[d], top_ref[...], d)
                    sum_ref[...] += sums
                    mixed_ref[...] += mixed

            gate = jnp.sum(jnp.where(level == level_of(c), gates, jnp.float32(0.0)), axis=0, keepdims=True)
            total = jnp.sum(sum_ref[...], axis=1, keepdims=True)
            mixed = mixed_ref[...] / total * gate
            mixed = jnp.where(place < count_of(c), mixed, jnp.float32(0.0))
            out_ref[c * per_group : (c + 1) * per_group] = mixed.astype(jnp.bfloat16).reshape(
                per_group, local, HEAD_DIM
            )

    @pl.when(busy == 0)
    def _():
        out_ref[...] = jnp.zeros_like(out_ref)


def head_each(queries, keys, values, counts, plan, group_mask, gate_table):
    axes = ("seq", "head")
    n_dev = lax.axis_size("seq") * lax.axis_size("head")
    local, feat = queries.shape
    heads = feat // HEAD_DIM
    parts = math.gcd(heads, n_dev)
    held, slots = heads // parts, n_dev // parts
    index = lax.axis_index("seq") * lax.axis_size("head") + lax.axis_index("head")
    lane = index % slots
    busy = (lane < held).astype(jnp.int32)
    head = jnp.minimum(index // slots * held + lane, heads - 1)
    place = jnp.stack([head, busy]).astype(jnp.int32)
    info = jnp.concatenate([place, counts, plan, group_mask.reshape(-1)])
    smem = pl.BlockSpec(memory_space=pltpu.SMEM)
    vmem = pl.BlockSpec(memory_space=pltpu.VMEM)

    sent = pack((queries, keys, values), parts, held, n_dev)
    got = lax.all_to_all(sent, axes, split_axis=0, concat_axis=0, tiled=True)
    rows = n_dev * local // GROUPS
    result = pl.pallas_call(
        attention_kernel,
        out_shape=jax.ShapeDtypeStruct((n_dev, local, HEAD_DIM), jnp.bfloat16),
        in_specs=[smem, vmem, vmem],
        out_specs=vmem,
        scratch_shapes=[
            pltpu.VMEM((GROUPS, rows, HEAD_DIM), jnp.bfloat16),
            pltpu.VMEM((GROUPS - 1, rows, rows), jnp.float32),
            pltpu.VMEM((rows, HEAD_DIM), jnp.float32),
            pltpu.VMEM((rows, HEAD_DIM), jnp.float32),
            pltpu.VMEM((rows, rows), jnp.float32),
            pltpu.VMEM((rows, rows), jnp.float32),
            pltpu.VMEM((rows, HEAD_DIM), jnp.float32),
            pltpu.VMEM((rows, HEAD_DIM), jnp.float32),
        ],
        compiler_params=pltpu.CompilerParams(vmem_limit_bytes=40 * 1024 * 1024),
        name="attention",
    )(info, got, gate_table)
    back = lax.all_to_all(result, axes, split_axis=0, concat_axis=0, tiled=True)
    return pl.pallas_call(
        functools.partial(unpack_kernel, parts, held),
        out_shape=jax.ShapeDtypeStruct((local, feat), jnp.bfloat16),
        in_specs=[vmem],
        out_specs=pl.BlockSpec(memory_space=pl.ANY),
        scratch_shapes=[pltpu.SemaphoreType.DMA],
        compiler_params=pltpu.CompilerParams(vmem_limit_bytes=16 * 1024 * 1024),
        name="unpack",
    )(back)


def on_device(queries, keys, values, counts, plan, group_mask, gate_table):
    n_dev = lax.axis_size("seq") * lax.axis_size("head")
    heads = queries.shape[1] // HEAD_DIM
    plan_of = head_each if heads <= n_dev <= 2 * heads else gathered
    return plan_of(queries, keys, values, counts, plan, group_mask, gate_table)


def solution(mesh):
    in_specs = (
        P(("seq", "head"), None),
        P(("seq", "head"), None),
        P(("seq", "head"), None),
        P(),
        P(),
        P(),
        P(),
    )
    out_specs = P(("seq", "head"), None)
    return jax.shard_map(
        on_device, mesh=mesh, in_specs=in_specs, out_specs=out_specs, check_vma=False
    )
```

```python
import functools
import math

import jax
import jax.numpy as jnp
from jax import lax
from jax.experimental import pallas as pl
from jax.experimental.pallas import tpu as pltpu
from jax.sharding import PartitionSpec as P

HEAD_DIM = 128
GROUPS = 4
LEVELS = 8


def lookup(table, index):
    hits = index[:, None] == jnp.arange(table.shape[0], dtype=jnp.int32)[None, :]
    return jnp.sum(jnp.where(hits, table[None, :], 0), axis=1)


def attend(
    work_q, k_local, v_local, row_group, row_pos, counts, plan, group_mask, gate_slice, group_tok
):
    rows = work_q.shape[0]
    width = work_q.shape[1]
    heads_here = width // HEAD_DIM
    scale = 1.0 / math.sqrt(HEAD_DIM)
    q_three = work_q.reshape(rows, heads_here, HEAD_DIM)
    row_onehot = (row_group[:, None] == jnp.arange(GROUPS, dtype=jnp.int32)[None, :]).astype(
        jnp.float32
    )
    mask_rows = jnp.dot(row_onehot, group_mask.astype(jnp.float32))
    k_piece = lax.all_gather(k_local, "seq", axis=0, tiled=True)
    v_piece = lax.all_gather(v_local, "seq", axis=0, tiled=True)
    count = k_piece.shape[0]
    index = jnp.arange(count, dtype=jnp.int32)
    k_group = index // group_tok
    k_pos = index % group_tok
    k_onehot = (k_group[:, None] == jnp.arange(GROUPS, dtype=jnp.int32)[None, :]).astype(
        jnp.float32
    )
    k_valid = k_pos < lookup(counts, k_group)
    allowed = (jnp.dot(mask_rows, k_onehot.T) > 0.5) & k_valid[None, :]
    running = jnp.full((heads_here, rows), -1e30, jnp.float32)
    k_three = k_piece.reshape(count, heads_here, HEAD_DIM)
    v_three = v_piece.reshape(count, heads_here, HEAD_DIM)
    scores = (
        jnp.einsum("qhd,khd->hqk", q_three, k_three, preferred_element_type=jnp.float32) * scale
    )
    scores = jnp.where(allowed[None], scores, jnp.float32(-1e30))
    newest = jnp.maximum(running, jnp.max(scores, axis=2))
    weights = jnp.exp(scores - newest[:, :, None]) * allowed[None].astype(jnp.float32)
    total = jnp.sum(weights, axis=2)
    rounded = weights.astype(jnp.bfloat16)
    accum = jnp.einsum("hqk,khd->hqd", rounded, v_three, preferred_element_type=jnp.float32)
    running, total, accum = (newest, total, accum)
    mixed = accum / total[:, :, None]
    mixed = jnp.transpose(mixed, (1, 0, 2)).reshape(rows, width)
    level_rows = lookup(plan, row_group)
    level_hits = level_rows[:, None] == jnp.arange(LEVELS, dtype=jnp.int32)[None, :]
    gates = jnp.sum(
        jnp.where(level_hits[:, :, None], gate_slice[None, :, :], jnp.float32(0.0)), axis=1
    )
    live = row_pos < lookup(counts, row_group)
    return jnp.where(live[:, None], mixed * gates, jnp.float32(0.0)).astype(jnp.bfloat16)


def gathered(queries, keys, values, counts, plan, group_mask, gate_table):
    n_seq = lax.axis_size("seq")
    n_head = lax.axis_size("head")
    per_group = n_seq // GROUPS
    tok_dev = queries.shape[0] * n_head
    group_tok = tok_dev * per_group
    q_local, k_local, v_local = (
        lax.all_to_all(queries, "head", split_axis=1, concat_axis=0, tiled=True),
        lax.all_to_all(keys, "head", split_axis=1, concat_axis=0, tiled=True),
        lax.all_to_all(values, "head", split_axis=1, concat_axis=0, tiled=True),
    )
    width = q_local.shape[1]
    seq_index = lax.axis_index("seq")
    own_group = seq_index // per_group
    positions = seq_index % per_group * tok_dev + jnp.arange(tok_dev, dtype=jnp.int32)
    gate_slice = lax.dynamic_slice_in_dim(gate_table, lax.axis_index("head") * width, width, 1)
    row_group = jnp.full((tok_dev,), own_group, jnp.int32)
    result = attend(
        q_local,
        k_local,
        v_local,
        row_group,
        positions,
        counts,
        plan,
        group_mask,
        gate_slice,
        group_tok,
    )
    return lax.all_to_all(result, "head", split_axis=0, concat_axis=1, tiled=True)


def pack_kernel(parts, held, q_ref, k_ref, v_ref, out_ref, in_buf, out_buf, in_sem, out_sem):
    slots = out_ref.shape[0] // parts
    arrays = (q_ref, k_ref, v_ref)
    copies = [pltpu.make_async_copy(ref, in_buf.at[i], in_sem.at[i]) for i, ref in enumerate(arrays)]
    for copy in copies:
        copy.start()
    for s in range(held, slots):
        for p in range(parts):
            for i in range(len(arrays)):
                out_buf[i, p * slots + s] = jnp.zeros(out_buf.shape[2:], out_buf.dtype)
    stores = []
    for i, copy in enumerate(copies):
        copy.wait()
        for p in range(parts):
            for s in range(held):
                h = p * held + s
                out_buf[i, p * slots + s] = in_buf[i, :, h * HEAD_DIM : (h + 1) * HEAD_DIM]
        stores.append(pltpu.make_async_copy(out_buf.at[i], out_ref.at[:, i], out_sem.at[i]))
        stores[-1].start()
    for store in stores:
        store.wait()


def pack(arrays, parts, held, n_dev):
    local, feat = arrays[0].shape
    count = len(arrays)
    return pl.pallas_call(
        functools.partial(pack_kernel, parts, held),
        out_shape=jax.ShapeDtypeStruct((n_dev, count, local, HEAD_DIM), jnp.bfloat16),
        in_specs=[pl.BlockSpec(memory_space=pl.ANY)] * count,
        out_specs=pl.BlockSpec(memory_space=pl.ANY),
        scratch_shapes=[
            pltpu.VMEM((count, local, feat), jnp.bfloat16),
            pltpu.VMEM((count, n_dev, local, HEAD_DIM), jnp.bfloat16),
            pltpu.SemaphoreType.DMA((count,)),
            pltpu.SemaphoreType.DMA((count,)),
        ],
        compiler_params=pltpu.CompilerParams(vmem_limit_bytes=60 * 1024 * 1024),
        name="pack",
    )(*arrays)


def unpack_kernel(parts, held, in_ref, out_ref, sem):
    slots = in_ref.shape[0] // parts
    for p in range(parts):
        for s in range(held):
            h = p * held + s
            pltpu.make_async_copy(
                in_ref.at[p * slots + s], out_ref.at[:, h * HEAD_DIM : (h + 1) * HEAD_DIM], sem
            ).start()
    pltpu.make_async_copy(out_ref, out_ref, sem).wait()


def attention_kernel(
    info_ref, got_ref, gate_ref, out_ref, score_ref, mixed_ref, sum_ref, *pair_refs
):
    n_dev, _, local, _ = got_ref.shape
    per_group = n_dev // GROUPS
    rows = per_group * local
    factor = 1.0 / math.sqrt(HEAD_DIM)
    own_refs, top_refs = pair_refs[:2], pair_refs[2:]
    head = info_ref[0]
    busy = info_ref[1]

    def count_of(group):
        return info_ref[2 + group]

    def level_of(group):
        return info_ref[2 + GROUPS + group]

    def sees(group, other):
        return info_ref[2 + 2 * GROUPS + group * GROUPS + other] == 1

    @pl.when(busy == 1)
    def _():
        gates = gate_ref[:, pl.ds(pl.multiple_of(head * HEAD_DIM, HEAD_DIM), HEAD_DIM)]
        level = lax.broadcasted_iota(jnp.int32, (LEVELS, HEAD_DIM), 0)
        place = lax.broadcasted_iota(jnp.int32, (rows, HEAD_DIM), 0)
        column = rows // 2 + lax.broadcasted_iota(jnp.int32, (1, rows // 2), 1)

        def part(group, kind):
            return got_ref[pl.ds(group * per_group, per_group), kind].reshape(rows, HEAD_DIM)

        def score(c, d):
            scores = lax.dot_general(
                part(c, 0), part(d, 1), (((1,), (1,)), ((), ())), preferred_element_type=jnp.float32
            )
            late = jnp.where(column < count_of(d), scores[:, rows // 2 :], jnp.float32(-1e30))
            return jnp.concatenate([scores[:, : rows // 2], late], axis=1)

        def lane_top(scores, top):
            pieces = [scores[:, i : i + HEAD_DIM] for i in range(0, rows, HEAD_DIM)]
            return functools.reduce(jnp.maximum, pieces, top)

        def product(scores, top, d):
            shift = jnp.concatenate([top] * (rows // HEAD_DIM), axis=1)
            weights = jnp.exp(scores * factor - shift)
            pieces = [weights[:, i : i + HEAD_DIM] for i in range(0, rows, HEAD_DIM)]
            return functools.reduce(jnp.add, pieces), jnp.dot(
                weights.astype(jnp.bfloat16), part(d, 2), preferred_element_type=jnp.float32
            )

        def own_scores(c):
            scores = score(c, c)
            own_refs[c % 2][...] = scores
            top_refs[c % 2][...] = lane_top(scores, jnp.float32(-1e30))

        own_scores(0)
        for c in range(GROUPS):
            top_ref = top_refs[c % 2]

            @pl.loop(0, c)
            def _(d):
                @pl.when(sees(c, d))
                def _():
                    scores = score(c, d)
                    score_ref[d] = scores
                    top_ref[...] = lane_top(scores, top_ref[...])

            top = jnp.max(top_ref[...], axis=1, keepdims=True) * factor
            top = jnp.broadcast_to(top, top_ref.shape)
            top_ref[...] = top
            if c + 1 < GROUPS:
                own_scores(c + 1)
            sum_ref[...], mixed_ref[...] = product(own_refs[c % 2][...], top, c)

            @pl.loop(0, c)
            def _(d):
                @pl.when(sees(c, d))
                def _():
                    sums, mixed = product(score_ref[d], top_ref[...], d)
                    sum_ref[...] += sums
                    mixed_ref[...] += mixed

            gate = jnp.sum(jnp.where(level == level_of(c), gates, jnp.float32(0.0)), axis=0, keepdims=True)
            total = jnp.sum(sum_ref[...], axis=1, keepdims=True)
            mixed = mixed_ref[...] / total * gate
            mixed = jnp.where(place < count_of(c), mixed, jnp.float32(0.0))
            out_ref[c * per_group : (c + 1) * per_group] = mixed.astype(jnp.bfloat16).reshape(
                per_group, local, HEAD_DIM
            )

    @pl.when(busy == 0)
    def _():
        out_ref[...] = jnp.zeros_like(out_ref)


def head_each(queries, keys, values, counts, plan, group_mask, gate_table):
    axes = ("seq", "head")
    n_dev = lax.axis_size("seq") * lax.axis_size("head")
    local, feat = queries.shape
    heads = feat // HEAD_DIM
    parts = math.gcd(heads, n_dev)
    held, slots = heads // parts, n_dev // parts
    index = lax.axis_index("seq") * lax.axis_size("head") + lax.axis_index("head")
    lane = index % slots
    busy = (lane < held).astype(jnp.int32)
    head = jnp.minimum(index // slots * held + lane, heads - 1)
    place = jnp.stack([head, busy]).astype(jnp.int32)
    info = jnp.concatenate([place, counts, plan, group_mask.reshape(-1)])
    smem = pl.BlockSpec(memory_space=pltpu.SMEM)
    vmem = pl.BlockSpec(memory_space=pltpu.VMEM)

    sent = pack((queries, keys, values), parts, held, n_dev)
    got = lax.all_to_all(sent, axes, split_axis=0, concat_axis=0, tiled=True)
    rows = n_dev * local // GROUPS
    result = pl.pallas_call(
        attention_kernel,
        out_shape=jax.ShapeDtypeStruct((n_dev, local, HEAD_DIM), jnp.bfloat16),
        in_specs=[smem, vmem, vmem],
        out_specs=vmem,
        scratch_shapes=[
            pltpu.VMEM((GROUPS - 1, rows, rows), jnp.float32),
            pltpu.VMEM((rows, HEAD_DIM), jnp.float32),
            pltpu.VMEM((rows, HEAD_DIM), jnp.float32),
            pltpu.VMEM((rows, rows), jnp.float32),
            pltpu.VMEM((rows, rows), jnp.float32),
            pltpu.VMEM((rows, HEAD_DIM), jnp.float32),
            pltpu.VMEM((rows, HEAD_DIM), jnp.float32),
        ],
        compiler_params=pltpu.CompilerParams(vmem_limit_bytes=40 * 1024 * 1024),
        name="attention",
    )(info, got, gate_table)
    back = lax.all_to_all(result, axes, split_axis=0, concat_axis=0, tiled=True)
    return pl.pallas_call(
        functools.partial(unpack_kernel, parts, held),
        out_shape=jax.ShapeDtypeStruct((local, feat), jnp.bfloat16),
        in_specs=[vmem],
        out_specs=pl.BlockSpec(memory_space=pl.ANY),
        scratch_shapes=[pltpu.SemaphoreType.DMA],
        compiler_params=pltpu.CompilerParams(vmem_limit_bytes=16 * 1024 * 1024),
        name="unpack",
    )(back)


def on_device(queries, keys, values, counts, plan, group_mask, gate_table):
    n_dev = lax.axis_size("seq") * lax.axis_size("head")
    heads = queries.shape[1] // HEAD_DIM
    plan_of = head_each if heads <= n_dev <= 2 * heads else gathered
    return plan_of(queries, keys, values, counts, plan, group_mask, gate_table)


def solution(mesh):
    in_specs = (
        P(("seq", "head"), None),
        P(("seq", "head"), None),
        P(("seq", "head"), None),
        P(),
        P(),
        P(),
        P(),
    )
    out_specs = P(("seq", "head"), None)
    return jax.shard_map(
        on_device, mesh=mesh, in_specs=in_specs, out_specs=out_specs, check_vma=False
    )
```

```python
import functools
import math

import jax
import jax.numpy as jnp
from jax import lax
from jax.experimental import pallas as pl
from jax.experimental.pallas import tpu as pltpu
from jax.sharding import PartitionSpec as P

HEAD_DIM = 128
GROUPS = 4
LEVELS = 8


def lookup(table, index):
    hits = index[:, None] == jnp.arange(table.shape[0], dtype=jnp.int32)[None, :]
    return jnp.sum(jnp.where(hits, table[None, :], 0), axis=1)


def attend(
    work_q, k_local, v_local, row_group, row_pos, counts, plan, group_mask, gate_slice, group_tok
):
    rows = work_q.shape[0]
    width = work_q.shape[1]
    heads_here = width // HEAD_DIM
    scale = 1.0 / math.sqrt(HEAD_DIM)
    q_three = work_q.reshape(rows, heads_here, HEAD_DIM)
    row_onehot = (row_group[:, None] == jnp.arange(GROUPS, dtype=jnp.int32)[None, :]).astype(
        jnp.float32
    )
    mask_rows = jnp.dot(row_onehot, group_mask.astype(jnp.float32))
    k_piece = lax.all_gather(k_local, "seq", axis=0, tiled=True)
    v_piece = lax.all_gather(v_local, "seq", axis=0, tiled=True)
    count = k_piece.shape[0]
    index = jnp.arange(count, dtype=jnp.int32)
    k_group = index // group_tok
    k_pos = index % group_tok
    k_onehot = (k_group[:, None] == jnp.arange(GROUPS, dtype=jnp.int32)[None, :]).astype(
        jnp.float32
    )
    k_valid = k_pos < lookup(counts, k_group)
    allowed = (jnp.dot(mask_rows, k_onehot.T) > 0.5) & k_valid[None, :]
    running = jnp.full((heads_here, rows), -1e30, jnp.float32)
    k_three = k_piece.reshape(count, heads_here, HEAD_DIM)
    v_three = v_piece.reshape(count, heads_here, HEAD_DIM)
    scores = (
        jnp.einsum("qhd,khd->hqk", q_three, k_three, preferred_element_type=jnp.float32) * scale
    )
    scores = jnp.where(allowed[None], scores, jnp.float32(-1e30))
    newest = jnp.maximum(running, jnp.max(scores, axis=2))
    weights = jnp.exp(scores - newest[:, :, None]) * allowed[None].astype(jnp.float32)
    total = jnp.sum(weights, axis=2)
    rounded = weights.astype(jnp.bfloat16)
    accum = jnp.einsum("hqk,khd->hqd", rounded, v_three, preferred_element_type=jnp.float32)
    running, total, accum = (newest, total, accum)
    mixed = accum / total[:, :, None]
    mixed = jnp.transpose(mixed, (1, 0, 2)).reshape(rows, width)
    level_rows = lookup(plan, row_group)
    level_hits = level_rows[:, None] == jnp.arange(LEVELS, dtype=jnp.int32)[None, :]
    gates = jnp.sum(
        jnp.where(level_hits[:, :, None], gate_slice[None, :, :], jnp.float32(0.0)), axis=1
    )
    live = row_pos < lookup(counts, row_group)
    return jnp.where(live[:, None], mixed * gates, jnp.float32(0.0)).astype(jnp.bfloat16)


def gathered(queries, keys, values, counts, plan, group_mask, gate_table):
    n_seq = lax.axis_size("seq")
    n_head = lax.axis_size("head")
    per_group = n_seq // GROUPS
    tok_dev = queries.shape[0] * n_head
    group_tok = tok_dev * per_group
    q_local, k_local, v_local = (
        lax.all_to_all(queries, "head", split_axis=1, concat_axis=0, tiled=True),
        lax.all_to_all(keys, "head", split_axis=1, concat_axis=0, tiled=True),
        lax.all_to_all(values, "head", split_axis=1, concat_axis=0, tiled=True),
    )
    width = q_local.shape[1]
    seq_index = lax.axis_index("seq")
    own_group = seq_index // per_group
    positions = seq_index % per_group * tok_dev + jnp.arange(tok_dev, dtype=jnp.int32)
    gate_slice = lax.dynamic_slice_in_dim(gate_table, lax.axis_index("head") * width, width, 1)
    row_group = jnp.full((tok_dev,), own_group, jnp.int32)
    result = attend(
        q_local,
        k_local,
        v_local,
        row_group,
        positions,
        counts,
        plan,
        group_mask,
        gate_slice,
        group_tok,
    )
    return lax.all_to_all(result, "head", split_axis=0, concat_axis=1, tiled=True)


def pack_kernel(parts, held, q_ref, k_ref, v_ref, out_ref, in_buf, out_buf, in_sem, out_sem):
    slots = out_ref.shape[0] // parts
    arrays = (q_ref, k_ref, v_ref)
    copies = [pltpu.make_async_copy(ref, in_buf.at[i], in_sem.at[i]) for i, ref in enumerate(arrays)]
    for copy in copies:
        copy.start()
    for s in range(held, slots):
        for p in range(parts):
            for i in range(len(arrays)):
                out_buf[i, p * slots + s] = jnp.zeros(out_buf.shape[2:], out_buf.dtype)
    stores = []
    for i, copy in enumerate(copies):
        copy.wait()
        for p in range(parts):
            for s in range(held):
                h = p * held + s
                out_buf[i, p * slots + s] = in_buf[i, :, h * HEAD_DIM : (h + 1) * HEAD_DIM]
        stores.append(pltpu.make_async_copy(out_buf.at[i], out_ref.at[:, i], out_sem.at[i]))
        stores[-1].start()
    for store in stores:
        store.wait()


def pack(arrays, parts, held, n_dev):
    local, feat = arrays[0].shape
    count = len(arrays)
    return pl.pallas_call(
        functools.partial(pack_kernel, parts, held),
        out_shape=jax.ShapeDtypeStruct((n_dev, count, local, HEAD_DIM), jnp.bfloat16),
        in_specs=[pl.BlockSpec(memory_space=pl.ANY)] * count,
        out_specs=pl.BlockSpec(memory_space=pl.ANY),
        scratch_shapes=[
            pltpu.VMEM((count, local, feat), jnp.bfloat16),
            pltpu.VMEM((count, n_dev, local, HEAD_DIM), jnp.bfloat16),
            pltpu.SemaphoreType.DMA((count,)),
            pltpu.SemaphoreType.DMA((count,)),
        ],
        compiler_params=pltpu.CompilerParams(vmem_limit_bytes=60 * 1024 * 1024),
        name="pack",
    )(*arrays)


def unpack_kernel(parts, held, in_ref, out_ref, sem):
    slots = in_ref.shape[0] // parts
    for p in range(parts):
        for s in range(held):
            h = p * held + s
            pltpu.make_async_copy(
                in_ref.at[p * slots + s], out_ref.at[:, h * HEAD_DIM : (h + 1) * HEAD_DIM], sem
            ).start()
    pltpu.make_async_copy(out_ref, out_ref, sem).wait()


def attention_kernel(
    info_ref, got_ref, gate_ref, out_ref, score_ref, mixed_ref, sum_ref, *pair_refs
):
    n_dev, _, local, _ = got_ref.shape
    per_group = n_dev // GROUPS
    rows = per_group * local
    factor = math.log2(math.e) / math.sqrt(HEAD_DIM)
    own_refs, top_refs = pair_refs[:2], pair_refs[2:]
    head = info_ref[0]
    busy = info_ref[1]

    def count_of(group):
        return info_ref[2 + group]

    def level_of(group):
        return info_ref[2 + GROUPS + group]

    def sees(group, other):
        return info_ref[2 + 2 * GROUPS + group * GROUPS + other] == 1

    @pl.when(busy == 1)
    def _():
        gates = gate_ref[:, pl.ds(pl.multiple_of(head * HEAD_DIM, HEAD_DIM), HEAD_DIM)]
        level = lax.broadcasted_iota(jnp.int32, (LEVELS, HEAD_DIM), 0)
        place = lax.broadcasted_iota(jnp.int32, (rows, HEAD_DIM), 0)
        column = rows // 2 + lax.broadcasted_iota(jnp.int32, (1, rows // 2), 1)

        def part(group, kind):
            return got_ref[pl.ds(group * per_group, per_group), kind].reshape(rows, HEAD_DIM)

        def score(c, d):
            scores = lax.dot_general(
                part(c, 0), part(d, 1), (((1,), (1,)), ((), ())), preferred_element_type=jnp.float32
            )
            late = jnp.where(column < count_of(d), scores[:, rows // 2 :], jnp.float32(-1e30))
            return jnp.concatenate([scores[:, : rows // 2], late], axis=1)

        def lane_top(scores, top):
            pieces = [scores[:, i : i + HEAD_DIM] for i in range(0, rows, HEAD_DIM)]
            return functools.reduce(jnp.maximum, pieces, top)

        def product(scores, top, d):
            shift = jnp.concatenate([top] * (rows // HEAD_DIM), axis=1)
            weights = jnp.exp2(scores * factor - shift)
            pieces = [weights[:, i : i + HEAD_DIM] for i in range(0, rows, HEAD_DIM)]
            return functools.reduce(jnp.add, pieces), jnp.dot(
                weights.astype(jnp.bfloat16), part(d, 2), preferred_element_type=jnp.float32
            )

        def own_scores(c):
            scores = score(c, c)
            own_refs[c % 2][...] = scores
            top_refs[c % 2][...] = lane_top(scores, jnp.float32(-1e30))

        own_scores(0)
        for c in range(GROUPS):
            top_ref = top_refs[c % 2]

            @pl.loop(0, c)
            def _(d):
                @pl.when(sees(c, d))
                def _():
                    scores = score(c, d)
                    score_ref[d] = scores
                    top_ref[...] = lane_top(scores, top_ref[...])

            top = jnp.max(top_ref[...], axis=1, keepdims=True) * factor
            top = jnp.broadcast_to(top, top_ref.shape)
            top_ref[...] = top
            if c + 1 < GROUPS:
                own_scores(c + 1)
            sum_ref[...], mixed_ref[...] = product(own_refs[c % 2][...], top, c)

            @pl.loop(0, c)
            def _(d):
                @pl.when(sees(c, d))
                def _():
                    sums, mixed = product(score_ref[d], top_ref[...], d)
                    sum_ref[...] += sums
                    mixed_ref[...] += mixed

            gate = jnp.sum(jnp.where(level == level_of(c), gates, jnp.float32(0.0)), axis=0, keepdims=True)
            total = jnp.sum(sum_ref[...], axis=1, keepdims=True)
            mixed = mixed_ref[...] / total * gate
            mixed = jnp.where(place < count_of(c), mixed, jnp.float32(0.0))
            out_ref[c * per_group : (c + 1) * per_group] = mixed.astype(jnp.bfloat16).reshape(
                per_group, local, HEAD_DIM
            )

    @pl.when(busy == 0)
    def _():
        out_ref[...] = jnp.zeros_like(out_ref)


def head_each(queries, keys, values, counts, plan, group_mask, gate_table):
    axes = ("seq", "head")
    n_dev = lax.axis_size("seq") * lax.axis_size("head")
    local, feat = queries.shape
    heads = feat // HEAD_DIM
    parts = math.gcd(heads, n_dev)
    held, slots = heads // parts, n_dev // parts
    index = lax.axis_index("seq") * lax.axis_size("head") + lax.axis_index("head")
    lane = index % slots
    busy = (lane < held).astype(jnp.int32)
    head = jnp.minimum(index // slots * held + lane, heads - 1)
    place = jnp.stack([head, busy]).astype(jnp.int32)
    info = jnp.concatenate([place, counts, plan, group_mask.reshape(-1)])
    smem = pl.BlockSpec(memory_space=pltpu.SMEM)
    vmem = pl.BlockSpec(memory_space=pltpu.VMEM)

    sent = pack((queries, keys, values), parts, held, n_dev)
    got = lax.all_to_all(sent, axes, split_axis=0, concat_axis=0, tiled=True)
    rows = n_dev * local // GROUPS
    result = pl.pallas_call(
        attention_kernel,
        out_shape=jax.ShapeDtypeStruct((n_dev, local, HEAD_DIM), jnp.bfloat16),
        in_specs=[smem, vmem, vmem],
        out_specs=vmem,
        scratch_shapes=[
            pltpu.VMEM((GROUPS - 1, rows, rows), jnp.float32),
            pltpu.VMEM((rows, HEAD_DIM), jnp.float32),
            pltpu.VMEM((rows, HEAD_DIM), jnp.float32),
            pltpu.VMEM((rows, rows), jnp.float32),
            pltpu.VMEM((rows, rows), jnp.float32),
            pltpu.VMEM((rows, HEAD_DIM), jnp.float32),
            pltpu.VMEM((rows, HEAD_DIM), jnp.float32),
        ],
        compiler_params=pltpu.CompilerParams(vmem_limit_bytes=40 * 1024 * 1024),
        name="attention",
    )(info, got, gate_table)
    back = lax.all_to_all(result, axes, split_axis=0, concat_axis=0, tiled=True)
    return pl.pallas_call(
        functools.partial(unpack_kernel, parts, held),
        out_shape=jax.ShapeDtypeStruct((local, feat), jnp.bfloat16),
        in_specs=[vmem],
        out_specs=pl.BlockSpec(memory_space=pl.ANY),
        scratch_shapes=[pltpu.SemaphoreType.DMA],
        compiler_params=pltpu.CompilerParams(vmem_limit_bytes=16 * 1024 * 1024),
        name="unpack",
    )(back)


def on_device(queries, keys, values, counts, plan, group_mask, gate_table):
    n_dev = lax.axis_size("seq") * lax.axis_size("head")
    heads = queries.shape[1] // HEAD_DIM
    plan_of = head_each if heads <= n_dev <= 2 * heads else gathered
    return plan_of(queries, keys, values, counts, plan, group_mask, gate_table)


def solution(mesh):
    in_specs = (
        P(("seq", "head"), None),
        P(("seq", "head"), None),
        P(("seq", "head"), None),
        P(),
        P(),
        P(),
        P(),
    )
    out_specs = P(("seq", "head"), None)
    return jax.shard_map(
        on_device, mesh=mesh, in_specs=in_specs, out_specs=out_specs, check_vma=False
    )
```

```python
import functools
import math

import jax
import jax.numpy as jnp
from jax import lax
from jax.experimental import pallas as pl
from jax.experimental.pallas import tpu as pltpu
from jax.sharding import PartitionSpec as P

HEAD_DIM = 128
GROUPS = 4
LEVELS = 8


def lookup(table, index):
    hits = index[:, None] == jnp.arange(table.shape[0], dtype=jnp.int32)[None, :]
    return jnp.sum(jnp.where(hits, table[None, :], 0), axis=1)


def attend(
    work_q, k_local, v_local, row_group, row_pos, counts, plan, group_mask, gate_slice, group_tok
):
    rows = work_q.shape[0]
    width = work_q.shape[1]
    heads_here = width // HEAD_DIM
    scale = 1.0 / math.sqrt(HEAD_DIM)
    q_three = work_q.reshape(rows, heads_here, HEAD_DIM)
    row_onehot = (row_group[:, None] == jnp.arange(GROUPS, dtype=jnp.int32)[None, :]).astype(
        jnp.float32
    )
    mask_rows = jnp.dot(row_onehot, group_mask.astype(jnp.float32))
    k_piece = lax.all_gather(k_local, "seq", axis=0, tiled=True)
    v_piece = lax.all_gather(v_local, "seq", axis=0, tiled=True)
    count = k_piece.shape[0]
    index = jnp.arange(count, dtype=jnp.int32)
    k_group = index // group_tok
    k_pos = index % group_tok
    k_onehot = (k_group[:, None] == jnp.arange(GROUPS, dtype=jnp.int32)[None, :]).astype(
        jnp.float32
    )
    k_valid = k_pos < lookup(counts, k_group)
    allowed = (jnp.dot(mask_rows, k_onehot.T) > 0.5) & k_valid[None, :]
    running = jnp.full((heads_here, rows), -1e30, jnp.float32)
    k_three = k_piece.reshape(count, heads_here, HEAD_DIM)
    v_three = v_piece.reshape(count, heads_here, HEAD_DIM)
    scores = (
        jnp.einsum("qhd,khd->hqk", q_three, k_three, preferred_element_type=jnp.float32) * scale
    )
    scores = jnp.where(allowed[None], scores, jnp.float32(-1e30))
    newest = jnp.maximum(running, jnp.max(scores, axis=2))
    weights = jnp.exp(scores - newest[:, :, None]) * allowed[None].astype(jnp.float32)
    total = jnp.sum(weights, axis=2)
    rounded = weights.astype(jnp.bfloat16)
    accum = jnp.einsum("hqk,khd->hqd", rounded, v_three, preferred_element_type=jnp.float32)
    running, total, accum = (newest, total, accum)
    mixed = accum / total[:, :, None]
    mixed = jnp.transpose(mixed, (1, 0, 2)).reshape(rows, width)
    level_rows = lookup(plan, row_group)
    level_hits = level_rows[:, None] == jnp.arange(LEVELS, dtype=jnp.int32)[None, :]
    gates = jnp.sum(
        jnp.where(level_hits[:, :, None], gate_slice[None, :, :], jnp.float32(0.0)), axis=1
    )
    live = row_pos < lookup(counts, row_group)
    return jnp.where(live[:, None], mixed * gates, jnp.float32(0.0)).astype(jnp.bfloat16)


def gathered(queries, keys, values, counts, plan, group_mask, gate_table):
    n_seq = lax.axis_size("seq")
    n_head = lax.axis_size("head")
    per_group = n_seq // GROUPS
    tok_dev = queries.shape[0] * n_head
    group_tok = tok_dev * per_group
    q_local, k_local, v_local = (
        lax.all_to_all(queries, "head", split_axis=1, concat_axis=0, tiled=True),
        lax.all_to_all(keys, "head", split_axis=1, concat_axis=0, tiled=True),
        lax.all_to_all(values, "head", split_axis=1, concat_axis=0, tiled=True),
    )
    width = q_local.shape[1]
    seq_index = lax.axis_index("seq")
    own_group = seq_index // per_group
    positions = seq_index % per_group * tok_dev + jnp.arange(tok_dev, dtype=jnp.int32)
    gate_slice = lax.dynamic_slice_in_dim(gate_table, lax.axis_index("head") * width, width, 1)
    row_group = jnp.full((tok_dev,), own_group, jnp.int32)
    result = attend(
        q_local,
        k_local,
        v_local,
        row_group,
        positions,
        counts,
        plan,
        group_mask,
        gate_slice,
        group_tok,
    )
    return lax.all_to_all(result, "head", split_axis=0, concat_axis=1, tiled=True)


def pack_kernel(parts, held, q_ref, k_ref, v_ref, out_ref, in_buf, out_buf, in_sem, out_sem):
    slots = out_ref.shape[0] // parts
    arrays = (q_ref, k_ref, v_ref)
    half = q_ref.shape[0] // 2
    pieces = [(i, pl.ds(r * half, half)) for i in range(len(arrays)) for r in range(2)]
    copies = [
        pltpu.make_async_copy(arrays[i].at[r], in_buf.at[i, r], in_sem.at[n]) for n, (i, r) in enumerate(pieces)
    ]
    for copy in copies:
        copy.start()
    for s in range(held, slots):
        for p in range(parts):
            for i in range(len(arrays)):
                out_buf[i, p * slots + s] = jnp.zeros(out_buf.shape[2:], out_buf.dtype)
    stores = []
    for n, (i, r) in enumerate(pieces):
        copies[n].wait()
        for p in range(parts):
            for s in range(held):
                h = p * held + s
                out_buf[i, p * slots + s, r] = in_buf[i, r, h * HEAD_DIM : (h + 1) * HEAD_DIM]
        stores.append(pltpu.make_async_copy(out_buf.at[i, :, r], out_ref.at[:, i, r], out_sem.at[n]))
        stores[-1].start()
    for store in stores:
        store.wait()


def pack(arrays, parts, held, n_dev):
    local, feat = arrays[0].shape
    count = len(arrays)
    return pl.pallas_call(
        functools.partial(pack_kernel, parts, held),
        out_shape=jax.ShapeDtypeStruct((n_dev, count, local, HEAD_DIM), jnp.bfloat16),
        in_specs=[pl.BlockSpec(memory_space=pl.ANY)] * count,
        out_specs=pl.BlockSpec(memory_space=pl.ANY),
        scratch_shapes=[
            pltpu.VMEM((count, local, feat), jnp.bfloat16),
            pltpu.VMEM((count, n_dev, local, HEAD_DIM), jnp.bfloat16),
            pltpu.SemaphoreType.DMA((2 * count,)),
            pltpu.SemaphoreType.DMA((2 * count,)),
        ],
        compiler_params=pltpu.CompilerParams(vmem_limit_bytes=60 * 1024 * 1024),
        name="pack",
    )(*arrays)


def unpack_kernel(parts, held, in_ref, out_ref, sem):
    slots = in_ref.shape[0] // parts
    for p in range(parts):
        for s in range(held):
            h = p * held + s
            pltpu.make_async_copy(
                in_ref.at[p * slots + s], out_ref.at[:, h * HEAD_DIM : (h + 1) * HEAD_DIM], sem
            ).start()
    pltpu.make_async_copy(out_ref, out_ref, sem).wait()


def attention_kernel(
    info_ref, got_ref, gate_ref, out_ref, score_ref, mixed_ref, sum_ref, *pair_refs
):
    n_dev, _, local, _ = got_ref.shape
    per_group = n_dev // GROUPS
    rows = per_group * local
    factor = 1.0 / math.sqrt(HEAD_DIM)
    own_refs, top_refs = pair_refs[:2], pair_refs[2:]
    head = info_ref[0]
    busy = info_ref[1]

    def count_of(group):
        return info_ref[2 + group]

    def level_of(group):
        return info_ref[2 + GROUPS + group]

    def sees(group, other):
        return info_ref[2 + 2 * GROUPS + group * GROUPS + other] == 1

    @pl.when(busy == 1)
    def _():
        gates = gate_ref[:, pl.ds(pl.multiple_of(head * HEAD_DIM, HEAD_DIM), HEAD_DIM)]
        level = lax.broadcasted_iota(jnp.int32, (LEVELS, HEAD_DIM), 0)
        place = lax.broadcasted_iota(jnp.int32, (rows, HEAD_DIM), 0)
        column = rows // 2 + lax.broadcasted_iota(jnp.int32, (1, rows // 2), 1)

        def part(group, kind):
            return got_ref[pl.ds(group * per_group, per_group), kind].reshape(rows, HEAD_DIM)

        def score(c, d):
            scores = lax.dot_general(
                part(c, 0), part(d, 1), (((1,), (1,)), ((), ())), preferred_element_type=jnp.float32
            )
            late = jnp.where(column < count_of(d), scores[:, rows // 2 :], jnp.float32(-1e30))
            return jnp.concatenate([scores[:, : rows // 2], late], axis=1)

        def lane_top(scores, top):
            pieces = [scores[:, i : i + HEAD_DIM] for i in range(0, rows, HEAD_DIM)]
            return functools.reduce(jnp.maximum, pieces, top)

        def product(scores, top, d):
            shift = jnp.concatenate([top] * (rows // HEAD_DIM), axis=1)
            weights = jnp.exp(scores * factor - shift)
            pieces = [weights[:, i : i + HEAD_DIM] for i in range(0, rows, HEAD_DIM)]
            return functools.reduce(jnp.add, pieces), jnp.dot(
                weights.astype(jnp.bfloat16), part(d, 2), preferred_element_type=jnp.float32
            )

        def own_scores(c):
            scores = score(c, c)
            own_refs[c % 2][...] = scores
            top_refs[c % 2][...] = lane_top(scores, jnp.float32(-1e30))

        own_scores(0)
        for c in range(GROUPS):
            top_ref = top_refs[c % 2]

            @pl.loop(0, c)
            def _(d):
                @pl.when(sees(c, d))
                def _():
                    scores = score(c, d)
                    score_ref[d] = scores
                    top_ref[...] = lane_top(scores, top_ref[...])

            top = jnp.max(top_ref[...], axis=1, keepdims=True) * factor
            top = jnp.broadcast_to(top, top_ref.shape)
            top_ref[...] = top
            if c + 1 < GROUPS:
                own_scores(c + 1)
            sum_ref[...], mixed_ref[...] = product(own_refs[c % 2][...], top, c)

            @pl.loop(0, c)
            def _(d):
                @pl.when(sees(c, d))
                def _():
                    sums, mixed = product(score_ref[d], top_ref[...], d)
                    sum_ref[...] += sums
                    mixed_ref[...] += mixed

            gate = jnp.sum(jnp.where(level == level_of(c), gates, jnp.float32(0.0)), axis=0, keepdims=True)
            total = jnp.sum(sum_ref[...], axis=1, keepdims=True)
            mixed = mixed_ref[...] / total * gate
            mixed = jnp.where(place < count_of(c), mixed, jnp.float32(0.0))
            out_ref[c * per_group : (c + 1) * per_group] = mixed.astype(jnp.bfloat16).reshape(
                per_group, local, HEAD_DIM
            )

    @pl.when(busy == 0)
    def _():
        out_ref[...] = jnp.zeros_like(out_ref)


def head_each(queries, keys, values, counts, plan, group_mask, gate_table):
    axes = ("seq", "head")
    n_dev = lax.axis_size("seq") * lax.axis_size("head")
    local, feat = queries.shape
    heads = feat // HEAD_DIM
    parts = math.gcd(heads, n_dev)
    held, slots = heads // parts, n_dev // parts
    index = lax.axis_index("seq") * lax.axis_size("head") + lax.axis_index("head")
    lane = index % slots
    busy = (lane < held).astype(jnp.int32)
    head = jnp.minimum(index // slots * held + lane, heads - 1)
    place = jnp.stack([head, busy]).astype(jnp.int32)
    info = jnp.concatenate([place, counts, plan, group_mask.reshape(-1)])
    smem = pl.BlockSpec(memory_space=pltpu.SMEM)
    vmem = pl.BlockSpec(memory_space=pltpu.VMEM)

    sent = pack((queries, keys, values), parts, held, n_dev)
    got = lax.all_to_all(sent, axes, split_axis=0, concat_axis=0, tiled=True)
    rows = n_dev * local // GROUPS
    result = pl.pallas_call(
        attention_kernel,
        out_shape=jax.ShapeDtypeStruct((n_dev, local, HEAD_DIM), jnp.bfloat16),
        in_specs=[smem, vmem, vmem],
        out_specs=vmem,
        scratch_shapes=[
            pltpu.VMEM((GROUPS - 1, rows, rows), jnp.float32),
            pltpu.VMEM((rows, HEAD_DIM), jnp.float32),
            pltpu.VMEM((rows, HEAD_DIM), jnp.float32),
            pltpu.VMEM((rows, rows), jnp.float32),
            pltpu.VMEM((rows, rows), jnp.float32),
            pltpu.VMEM((rows, HEAD_DIM), jnp.float32),
            pltpu.VMEM((rows, HEAD_DIM), jnp.float32),
        ],
        compiler_params=pltpu.CompilerParams(vmem_limit_bytes=40 * 1024 * 1024),
        name="attention",
    )(info, got, gate_table)
    back = lax.all_to_all(result, axes, split_axis=0, concat_axis=0, tiled=True)
    return pl.pallas_call(
        functools.partial(unpack_kernel, parts, held),
        out_shape=jax.ShapeDtypeStruct((local, feat), jnp.bfloat16),
        in_specs=[vmem],
        out_specs=pl.BlockSpec(memory_space=pl.ANY),
        scratch_shapes=[pltpu.SemaphoreType.DMA],
        compiler_params=pltpu.CompilerParams(vmem_limit_bytes=16 * 1024 * 1024),
        name="unpack",
    )(back)


def on_device(queries, keys, values, counts, plan, group_mask, gate_table):
    n_dev = lax.axis_size("seq") * lax.axis_size("head")
    heads = queries.shape[1] // HEAD_DIM
    plan_of = head_each if heads <= n_dev <= 2 * heads else gathered
    return plan_of(queries, keys, values, counts, plan, group_mask, gate_table)


def solution(mesh):
    in_specs = (
        P(("seq", "head"), None),
        P(("seq", "head"), None),
        P(("seq", "head"), None),
        P(),
        P(),
        P(),
        P(),
    )
    out_specs = P(("seq", "head"), None)
    return jax.shard_map(
        on_device, mesh=mesh, in_specs=in_specs, out_specs=out_specs, check_vma=False
    )
```
